256 devices in a mesh: replica: 16 (over y_lo, z), shard: 16 (over y_hi, x, core).
Axes of the slice: x: 4, y: 4 (y_hi: 2, y_lo: 2; y = y_hi * 2 + y_lo), z: 8, core: 2. Of those that a mesh axis runs over, the one named last changes fastest.
Arguments:
- grad_key: bfloat16 [16, 1024, 8192], P('replica', 'shard')
- error_key: bfloat16 [16, 1024, 8192], P('replica', 'shard'), may hold values from -3 to 3
- prev_key: bfloat16 [8192, 64], P('shard'), may hold values from -6 to 6
- grad_val: bfloat16 [16, 1024, 8192], P('replica', 'shard')
- error_val: bfloat16 [16, 1024, 8192], P('replica', 'shard'), may hold values from -3 to 3
- prev_val: bfloat16 [8192, 64], P('shard'), may hold values from -6 to 6
Outputs:
- update_key: bfloat16 [1024, 8192], P('shard')
- next_error_key: bfloat16 [16, 1024, 8192], P('replica', 'shard')
- factor_key: float32 [8192, 64], P('shard')
- update_val: bfloat16 [1024, 8192], P('shard')
- next_error_val: bfloat16 [16, 1024, 8192], P('replica', 'shard')
- factor_val: float32 [8192, 64], P('shard')
The draws below stay inside these ranges and needn't reach their ends.
All inputs are finite; a program needn't handle non-finite values.
Results may differ from the reference program's by a relative error of at most 0.012.
Values may be sent and summed in bfloat16 or wider, within the bound.
A program may use at most 64 MiB of HBM per device.

```python
import jax
import jax.numpy as jnp
from jax import lax

COLS = 8192
KV_WIDTH = 1024
RANK = 64
N_REPLICA = 16


def rough_grads(key, row_count, share):
    key_rows, key_cols, key_common, key_own = jax.random.split(key, 4)
    row_scale = jnp.exp(jax.random.uniform(key_rows, (1, row_count, 1), jnp.float32, -1.15, 1.15))
    ramp = 0.6 + 1.2 * jnp.arange(row_count, dtype=jnp.float32)[None, :, None] / row_count
    col_scale = jnp.exp(jax.random.uniform(key_cols, (1, 1, COLS), jnp.float32, -1.15, 1.15))
    common = jax.random.normal(key_common, (1, row_count, COLS), jnp.float32)
    own = jax.random.normal(key_own, (N_REPLICA, row_count, COLS), jnp.float32)
    mixed = (share * common + own) / jnp.sqrt(1.0 + share * share)
    return (0.5 * mixed * row_scale * ramp * col_scale).astype(jnp.bfloat16)


def draw_grad_key(key, part):
    key = jax.random.fold_in(key, 11)
    share = 0.7
    return rough_grads(key, KV_WIDTH, share)


def draw_grad_val(key, part):
    key = jax.random.fold_in(key, 23)
    share = 0.7
    return rough_grads(key, KV_WIDTH, share)


def shard_levels(stream_key, extent, shards, least, high):
    level = 1.0
    for dim, parts in shards:
        draws = jax.random.uniform(jax.random.fold_in(jax.random.fold_in(stream_key, 6), dim), (parts,), jnp.float32, least / len(shards), high / len(shards))
        level = level * jnp.repeat(jnp.exp(draws), extent[dim] // parts).reshape((-1,) + (1,) * (len(extent) - 1 - dim))
    return level


def bell_draw(rng, extent, scale, limit, shards=(), held_as=jnp.bfloat16):
    values = scale * jax.random.normal(rng, extent, jnp.float32)
    if shards:
        values = values * shard_levels(rng, extent, shards, -0.22, 0.18)
    return jnp.clip(values, -limit, limit).astype(held_as)


def setup_inputs(seed: int = 0) -> dict:
    keys = jax.random.split(jax.random.key(seed), 7)
    grad_key = draw_grad_key(jax.random.fold_in(keys[6], 71), 0)
    error_key = bell_draw(keys[1], (N_REPLICA, KV_WIDTH, COLS), 0.5, 3.0, ((0, 16), (1, 16)))
    prev_key = bell_draw(keys[2], (COLS, RANK), 1.0, 6.0, ((0, 16),))
    grad_val = draw_grad_val(jax.random.fold_in(keys[6], 71), 0)
    error_val = bell_draw(keys[4], (N_REPLICA, KV_WIDTH, COLS), 0.5, 3.0, ((0, 16), (1, 16)))
    prev_val = bell_draw(keys[5], (COLS, RANK), 1.0, 6.0, ((0, 16),))
    return dict(grad_key=grad_key, error_key=error_key, prev_key=prev_key, grad_val=grad_val, error_val=error_val, prev_val=prev_val)


def compress(grads, errors, previous):
    replicas = grads.shape[0]
    row_count = grads.shape[1]
    col_count = grads.shape[2]
    merged = (grads.astype(jnp.float32) + errors.astype(jnp.float32)).astype(jnp.bfloat16)
    flat = merged.reshape(replicas * row_count, col_count)
    partial_value = jnp.dot(flat.astype(jnp.float32), previous.astype(jnp.float32), preferred_element_type=jnp.float32)
    left = jnp.sum(partial_value.reshape(replicas, row_count, -1), axis=0) / replicas
    rank_size = left.shape[1]
    gram = jnp.dot(left.T, left, precision=lax.Precision.HIGHEST)
    ridged = gram + 1e-06 * (jnp.trace(gram) / rank_size) * jnp.eye(rank_size, dtype=jnp.float32)
    lower = jnp.linalg.cholesky(ridged)
    ortho = lax.linalg.triangular_solve(lower, left, left_side=False, lower=True, transpose_a=True)
    ortho_b = ortho.astype(jnp.bfloat16)
    stacked = jnp.tile(ortho_b, (replicas, 1))
    factor = jnp.dot(flat.T.astype(jnp.float32), stacked.astype(jnp.float32), preferred_element_type=jnp.float32) / replicas
    factor_b = factor.astype(jnp.bfloat16)
    approx = jnp.dot(ortho_b.astype(jnp.float32), factor_b.T.astype(jnp.float32), preferred_element_type=jnp.float32)
    update = approx.astype(jnp.bfloat16)
    next_error = (merged.astype(jnp.float32) - approx[None]).astype(jnp.bfloat16)
    return (update, next_error, factor)

def reference(grad_key, error_key, prev_key, grad_val, error_val, prev_val):
    update_key, next_error_key, factor_key = compress(grad_key, error_key, prev_key)
    update_val, next_error_val, factor_val = compress(grad_val, error_val, prev_val)
    return (update_key, next_error_key, factor_key, update_val, next_error_val, factor_val)
```

```python
import functools

import jax
import jax.numpy as jnp
from jax import lax
from jax.experimental import pallas as pl
from jax.experimental.pallas import tpu as pltpu
from jax.sharding import PartitionSpec as P

MESH = pl.DeviceIdType.MESH
F32, BF16 = jnp.float32, jnp.bfloat16
NX, NY, NZ, NC = 4, 4, 8, 2
REPLICAS = 16
RANK = 64
ROWS = 64
BLK = 512
BLKS = 16
RIDGE = 1e-6
NT = (((1,), (1,)), ((), ()))
NN = (((1,), (0,)), ((), ()))


def device(x, y, z, c):
    return (lax.rem(y, 2) * NZ + z, (lax.div(y, 2) * NX + x) * NC + c)


def send(src, dst, ssem, rsem, dev):
    copy = pltpu.make_async_remote_copy(
        src_ref=src, dst_ref=dst, send_sem=ssem, recv_sem=rsem, device_id=dev, device_id_type=MESH
    )
    copy.start()
    return copy


def arrival(dst, ssem, rsem, dev):
    pltpu.make_async_remote_copy(
        src_ref=dst, dst_ref=dst, send_sem=ssem, recv_sem=rsem, device_id=dev, device_id_type=MESH
    ).wait_recv()


def lanes_low(shape):
    return lax.broadcasted_iota(jnp.int32, shape, 1) < RANK


def solve_rows(gram, left):
    shape = (RANK, 128)
    row = lax.broadcasted_iota(jnp.int32, shape, 0)
    lane = lax.broadcasted_iota(jnp.int32, shape, 1)
    low = lane < RANK
    swapped = pltpu.roll(left, RANK, 1)
    out = []
    for side in range(2):
        here = low if side == 0 else jnp.logical_not(low)
        diag = lane == row + side * RANK
        trace = jnp.sum(jnp.where(diag, gram, 0.0))
        ridge = RIDGE * (trace / RANK)
        whole = jnp.where(here, gram + jnp.where(diag, ridge, 0.0), swapped)
        out.append([whole[8 * t : 8 * t + 8] for t in range(8)])
    sub = lax.broadcasted_iota(jnp.int32, (8, 128), 0)
    for j in range(RANK - 1):
        top, pos = divmod(j, 8)
        for side in range(2):
            tiles = out[side]
            col = side * RANK + j
            pivot_row = tiles[top][pos : pos + 1, :]
            inv = 1.0 / pivot_row[:, col : col + 1]
            scaled = pivot_row * inv
            for t in range(top, 8):
                if t == top:
                    if pos == 7:
                        continue
                    factor = jnp.where(sub > pos, jnp.broadcast_to(tiles[t][:, col : col + 1], (8, 128)), 0.0)
                else:
                    factor = tiles[t][:, col : col + 1]
                tiles[t] = tiles[t] - factor * scaled
    done = []
    for side in range(2):
        whole = jnp.concatenate(out[side], axis=0)
        diag = lane == row + side * RANK
        pivots = jnp.sum(jnp.where(diag, whole, 0.0), axis=1, keepdims=True)
        done.append(pltpu.roll(whole * lax.rsqrt(pivots), RANK, 1))
    return jnp.where(low, done[0], 0.0), jnp.where(low, 0.0, done[1])


def step_kernel(
    gk, ek, pk, gv, ev, pv,
    m_out, o_out, f_out,
    grads, errors, mbuf, pbuf, acc, lbuf, r1, lt2, gp, cpair, c1, cfull, obl,
    obuf, wbuf, pr, s1, r2, s2, r3, s3, r4, fbuf,
    load_sem, out_sem,
    a_ss, a_rs, af_ss, af_rs, b_ss, b_rs, b2_ss, b2_rs, c0_ss, c0_rs, c1_ss, c1_rs, c2_ss, c2_rs,
    e0_ss, e0_rs, e1_ss, e1_rs, e2_ss, e2_rs, e3_ss, e3_rs,
    g3_ss, g3_rs, g2_ss, g2_rs, g1_ss, g1_rs, g0_ss, g0_rs,
):
    r = lax.axis_index("replica")
    s = lax.axis_index("shard")
    y_lo, z = lax.div(r, NZ), lax.rem(r, NZ)
    y_hi, x, c = lax.div(s, NX * NC), lax.rem(lax.div(s, NC), NX), lax.rem(s, NC)
    y = 2 * y_hi + y_lo
    oc = 1 - c
    cross = lax.rem(y + 3 + 2 * y_lo, NY)
    flip = 2 * y_hi + 1 - y_lo
    mate = device(x, y, z, oc)

    def at_x(d):
        return lax.rem(x + d, NX)

    def at_y(d):
        return lax.rem(y + d, NY)

    def at_z(d):
        return lax.rem(z + d, NZ)

    loads = [
        pltpu.make_async_copy(gk.at[0], grads.at[0], load_sem.at[0]),
        pltpu.make_async_copy(ek.at[0], errors.at[0], load_sem.at[1]),
        pltpu.make_async_copy(gv.at[0], grads.at[1], load_sem.at[2]),
        pltpu.make_async_copy(ev.at[0], errors.at[1], load_sem.at[3]),
    ]
    own_prev = [
        pltpu.make_async_copy(pk, pbuf.at[s, pl.ds(0, RANK)], load_sem.at[4]),
        pltpu.make_async_copy(pv, pbuf.at[s, pl.ds(RANK, RANK)], load_sem.at[5]),
    ]
    for copy in own_prev + loads:
        copy.start()

    partners = [device(x, flip, at_z(d), c) for d in (4, 3, 5, 2, 6, 1, 7)]
    partners += [device(x, y, at_z(d), c) for d in (4, 3, 5, 2, 6, 1, 7)]
    partners += [device(at_x(d), cross, z, c) for d in (2, 1, 3)]
    partners += [device(at_x(d), y, z, c) for d in (2, 1, 3)]
    partners += [device(x, at_y(d), z, c) for d in (2, 1, 3)]
    partners += [mate]
    barrier = pltpu.get_barrier_semaphore()
    for dev in partners:
        pl.semaphore_signal(barrier, inc=1, device_id=dev, device_id_type=MESH)
    for copy in own_prev:
        copy.wait()
    pl.semaphore_wait(barrier, len(partners))

    sent = []

    far = [(2, 1), (1, 1), (3, 1), (2, 0), (1, 0), (3, 0), (0, 1)]
    for i, (dx, over) in enumerate(far):
        dev = device(at_x(dx), cross if over else y, z, c)
        sent.append(send(pbuf.at[s], pbuf.at[s], a_ss.at[i], a_rs.at[i], dev))
    sent.append(send(pbuf.at[s], pbuf.at[s], af_ss.at[7], af_rs.at[7], mate))

    for copy in loads:
        copy.wait()

    def merge(b, carry):
        cols = pl.ds(pl.multiple_of(b * BLK, BLK), BLK)
        for m in range(2):
            total = grads[m, :, cols].astype(F32) + errors[m, :, cols].astype(F32)
            mbuf[b, m * ROWS : (m + 1) * ROWS, :] = total.astype(BF16)
        return carry

    lax.fori_loop(0, BLKS, merge, 0)
    store_m = pltpu.make_async_copy(mbuf, m_out, out_sem.at[0])
    store_m.start()

    def left_term(slot):
        return lax.dot_general(pbuf[slot], mbuf[slot], NT, preferred_element_type=F32)

    acc[...] = left_term(s)
    order = (6, 4, 5, 3, 1, 2, 0)
    slots = []
    for i, (dx, over) in enumerate(far):
        yy = (1 - y_hi) if over else y_hi
        slots.append((yy * NX + lax.rem(x + NX - dx, NX)) * NC)
    for i in order:
        slot = slots[i] + c
        arrival(pbuf.at[slot], a_ss.at[i], a_rs.at[i], mate)
        sent.append(send(pbuf.at[slot], pbuf.at[slot], af_ss.at[i], af_rs.at[i], mate))
        acc[...] += left_term(slot)
    for i in (7,) + order:
        slot = (s + oc - c) if i == 7 else slots[i] + oc
        arrival(pbuf.at[slot], af_ss.at[i], af_rs.at[i], mate)
        acc[...] += left_term(slot)

    low64 = lanes_low((RANK, 128))
    part = jnp.where(low64, acc[0:RANK, :], acc[RANK:, :])
    for t in range(NZ):
        lbuf[t] = part[8 * t : 8 * t + 8]
    r1[r] = lbuf[z]
    peers = [(1, d) for d in (4, 3, 5, 2, 6, 1, 7, 0)] + [(0, d) for d in (4, 3, 5, 2, 6, 1, 7)]
    for i, (over, dz) in enumerate(peers):
        dev = device(x, flip if over else y, at_z(dz), c)
        sent.append(send(lbuf.at[at_z(dz)], r1.at[r], b_ss.at[i], b_rs.at[i], dev))
    for i, (over, dz) in enumerate(peers):
        slot = ((1 - y_lo) if over else y_lo) * NZ + lax.rem(z + NZ - dz, NZ)
        arrival(r1.at[slot], b_ss.at[i], b_rs.at[i], mate)
    total = r1[0]
    for t in range(1, REPLICAS):
        total = total + r1[t]
    lt2[z] = total / REPLICAS
    zs = (4, 3, 5, 2, 6, 1, 7)
    for i, dz in enumerate(zs):
        sent.append(send(lt2.at[z], lt2.at[z], b2_ss.at[i], b2_rs.at[i], device(x, y, at_z(dz), c)))
    for i, dz in enumerate(zs):
        arrival(lt2.at[lax.rem(z + NZ - dz, NZ)], b2_ss.at[i], b2_rs.at[i], mate)

    left = jnp.concatenate([lt2[t] for t in range(NZ)], axis=0)
    wide = jnp.concatenate([jnp.where(low64, left, 0.0), jnp.where(low64, 0.0, left)], axis=0)
    gram = lax.dot_general(wide, wide, NT, precision=lax.Precision.HIGHEST, preferred_element_type=F32)
    gram = jnp.where(low64, gram[0:RANK], gram[RANK:])
    gp[0] = gram[0:32]
    gp[1] = gram[32:64]
    copy = send(gp.at[oc], cpair, c0_ss, c0_rs, mate)
    copy.wait_recv()
    sent.append(copy)
    chip = y_hi * NX + x
    c1[chip] = gp[c] + cpair[...]
    for i, (dx, over) in enumerate(far):
        dev = device(at_x(dx), cross if over else y, z, c)
        sent.append(send(c1.at[chip], c1.at[chip], c1_ss.at[i], c1_rs.at[i], dev))
    for i, (dx, over) in enumerate(far):
        arrival(c1.at[lax.div(slots[i], NC)], c1_ss.at[i], c1_rs.at[i], mate)
    total = c1[0]
    for t in range(1, 8):
        total = total + c1[t]
    cfull[c] = total
    copy = send(cfull.at[c], cfull.at[c], c2_ss, c2_rs, mate)
    arrival(cfull.at[oc], c2_ss, c2_rs, mate)
    sent.append(copy)
    gram = jnp.concatenate([cfull[0], cfull[1]], axis=0)

    key_rows, val_rows = solve_rows(gram, left)
    obl[0] = key_rows.astype(BF16)
    obl[1] = val_rows.astype(BF16)
    store_o = pltpu.make_async_copy(obl, o_out, out_sem.at[1])
    store_o.start()

    ordered = jnp.concatenate([obl[oc], obl[c]], axis=0)
    firsts = (x, y)
    seconds = (y, x)
    ds = (2, 1, 3, 0)

    def first(pq, d):
        return lax.rem(firsts[pq] + d, 4)

    def second(pq, d):
        return lax.rem(seconds[pq] + d, 4)

    def dev1(pq, d):
        return device(at_x(d), y, z, c) if pq == 0 else device(x, at_y(d), z, c)

    def dev2(pq, d):
        return device(x, at_y(d), z, c) if pq == 0 else device(at_x(d), y, z, c)

    pair_copies = {}
    for k, d in enumerate(ds):
        for pq in range(2):
            i1 = first(pq, d)
            for h in range(2):
                term = lax.dot_general(
                    ordered, mbuf[pq * 8 + i1 * 2 + h], NN, preferred_element_type=F32
                )
                for i in range(2):
                    for a in range(4):
                        for b in range(2):
                            cols = slice(i * 256 + b * 128, i * 256 + b * 128 + 128)
                            obuf[pq, i1, 2 * h + i, 2 * a + b] = term[16 * a : 16 * a + 16, cols].astype(BF16)
                            wbuf[pq, i1, 2 * h + i, 2 * a + b] = term[64 + 16 * a : 80 + 16 * a, cols]
            pair_copies[pq, k] = send(
                obuf.at[pq, i1], pr.at[pq, i1], e0_ss.at[pq, k], e0_rs.at[pq, k], mate
            )
    for k, d in enumerate(ds):
        for pq in range(2):
            i1 = first(pq, d)
            pair_copies[pq, k].wait_recv()
            sent.append(pair_copies[pq, k])
            total = wbuf[pq, i1] + pr[pq, i1].astype(F32)
            if d == 0:
                wbuf[pq, i1] = total
            else:
                s1[pq, k] = total.astype(BF16)
                sent.append(
                    send(s1.at[pq, k], r2.at[pq, k], e1_ss.at[pq, k], e1_rs.at[pq, k], dev1(pq, d))
                )
    for pq in range(2):
        for k in range(3):
            arrival(r2.at[pq, k], e1_ss.at[pq, k], e1_rs.at[pq, k], mate)
        i1 = first(pq, 0)
        for k, d in enumerate(ds):
            i2 = second(pq, d)
            total = wbuf[pq, i1, i2]
            for t in range(3):
                total = total + r2[pq, t, i2].astype(F32)
            if d == 0:
                wbuf[pq, i1, i2] = total
            else:
                s2[pq, k] = total.astype(BF16)
                sent.append(
                    send(s2.at[pq, k], r3.at[pq, k], e2_ss.at[pq, k], e2_rs.at[pq, k], dev2(pq, d))
                )
    for pq in range(2):
        for k in range(3):
            arrival(r3.at[pq, k], e2_ss.at[pq, k], e2_rs.at[pq, k], mate)
        i1, i2 = first(pq, 0), second(pq, 0)
        total = wbuf[pq, i1, i2]
        for t in range(3):
            total = total + r3[pq, t].astype(F32)
        wbuf[pq, i1, i2] = total
        s3[:, pq] = total.astype(BF16)
    for i, dz in enumerate(zs):
        there = at_z(dz)
        sent.append(send(s3.at[there], r4.at[i], e3_ss.at[i], e3_rs.at[i], device(x, y, there, c)))
    for i in range(7):
        arrival(r4.at[i], e3_ss.at[i], e3_rs.at[i], mate)
    for pq in range(2):
        i1, i2 = first(pq, 0), second(pq, 0)
        total = wbuf[pq, i1, i2, z]
        for i in range(7):
            total = total + r4[i, pq].astype(F32)
        fbuf[c, pq, i1, i2, z] = (total / REPLICAS).astype(BF16)

    for pq in range(2):
        piece = fbuf.at[c, pq, first(pq, 0), second(pq, 0), z]
        for i, dz in enumerate(zs):
            sent.append(send(piece, piece, g3_ss.at[pq, i], g3_rs.at[pq, i], device(x, y, at_z(dz), c)))
    for pq in range(2):
        i1, i2 = first(pq, 0), second(pq, 0)
        for i, dz in enumerate(zs):
            arrival(fbuf.at[c, pq, i1, i2, lax.rem(z + NZ - dz, NZ)], g3_ss.at[pq, i], g3_rs.at[pq, i], mate)
        piece = fbuf.at[c, pq, i1, i2]
        for k in range(3):
            sent.append(send(piece, piece, g2_ss.at[pq, k], g2_rs.at[pq, k], dev2(pq, ds[k])))
    for pq in range(2):
        i1 = first(pq, 0)
        for k in range(3):
            arrival(fbuf.at[c, pq, i1, second(pq, 4 - ds[k])], g2_ss.at[pq, k], g2_rs.at[pq, k], mate)
        piece = fbuf.at[c, pq, i1]
        for k in range(3):
            sent.append(send(piece, piece, g1_ss.at[pq, k], g1_rs.at[pq, k], dev1(pq, ds[k])))
        sent.append(send(piece, piece, g0_ss.at[pq, 3], g0_rs.at[pq, 3], mate))
    stores = []
    for k in (1, 2, 0):
        for pq in range(2):
            piece = fbuf.at[c, pq, first(pq, 4 - ds[k])]
            arrival(piece, g1_ss.at[pq, k], g1_rs.at[pq, k], mate)
            sent.append(send(piece, piece, g0_ss.at[pq, k], g0_rs.at[pq, k], mate))
    stores.append(pltpu.make_async_copy(fbuf.at[c], f_out.at[c], out_sem.at[2]))
    stores[-1].start()
    for k in (3, 1, 2, 0):
        for pq in range(2):
            piece = fbuf.at[oc, pq, first(pq, 4 - ds[k])]
            arrival(piece, g0_ss.at[pq, k], g0_rs.at[pq, k], mate)
    stores.append(pltpu.make_async_copy(fbuf.at[oc], f_out.at[oc], out_sem.at[3]))
    stores[-1].start()
    for copy in stores:
        copy.wait()
    store_m.wait()
    store_o.wait()
    for copy in sent:
        copy.wait_send()


def out_kernel(m_ref, o_ref, f_ref, uk, nk, uv, nv, fk, fv):
    s = lax.axis_index("shard")
    whole = jnp.concatenate([o_ref[0], o_ref[1]], axis=0)
    for i in range(4):
        sides = []
        for m in range(2):
            rows = [
                jnp.concatenate([f_ref[m, 0, 0, i, 2 * a], f_ref[m, 0, 0, i, 2 * a + 1]], axis=1)
                for a in range(4)
            ]
            sides.append(jnp.concatenate(rows, axis=0))
        factor = jnp.concatenate(sides, axis=0)
        approx = lax.dot_general(whole, factor, (((0,), (0,)), ((), ())), preferred_element_type=F32)
        cols = slice(256 * i, 256 * i + 256)
        merged = m_ref[i // 2, :, 256 * (i % 2) : 256 * (i % 2) + 256].astype(F32)
        rest = (merged - approx).astype(BF16)
        approx = approx.astype(BF16)
        uk[:, cols] = approx[:ROWS]
        uv[:, cols] = approx[ROWS:]
        nk[0, :, cols] = rest[:ROWS]
        nv[0, :, cols] = rest[ROWS:]

        @pl.when(jnp.logical_and(pl.program_id(0) == lax.div(s, 2), lax.rem(s, 2) == i // 2))
        def _():
            half = slice(256 * (i % 2), 256 * (i % 2) + 256)
            fk[:, half] = sides[0].astype(F32)
            fv[:, half] = sides[1].astype(F32)


def per_device(grad_key, error_key, prev_key, grad_val, error_val, prev_val):
    vm = pltpu.VMEM
    dma = pltpu.SemaphoreType.DMA
    scratch = [
        vm((2, ROWS, 8192), BF16), vm((2, ROWS, 8192), BF16),
        vm((BLKS, 128, BLK), BF16), vm((BLKS, 128, BLK), BF16),
        vm((128, 128), F32), vm((8, 8, 128), F32), vm((16, 8, 128), F32), vm((8, 8, 128), F32),
        vm((2, 32, 128), F32), vm((32, 128), F32), vm((8, 32, 128), F32), vm((2, 32, 128), F32),
        vm((2, RANK, 128), BF16),
        vm((2, 4, 4, 8, 16, 128), BF16), vm((2, 4, 4, 8, 16, 128), F32), vm((2, 4, 4, 8, 16, 128), BF16),
        vm((2, 3, 4, 8, 16, 128), BF16), vm((2, 3, 4, 8, 16, 128), BF16),
        vm((2, 3, 8, 16, 128), BF16), vm((2, 3, 8, 16, 128), BF16),
        vm((8, 2, 16, 128), BF16), vm((7, 2, 16, 128), BF16),
        vm((2, 2, 4, 4, 8, 16, 128), BF16),
        dma((6,)), dma((4,)),
    ]
    for n in ((7,), (8,), (15,), (7,), None, (7,), None, (2, 4), (2, 3), (2, 3), (7,), (2, 7), (2, 3), (2, 3), (2, 4)):
        for _ in range(2):
            scratch.append(dma if n is None else dma(n))
    hbm = pl.BlockSpec(memory_space=pl.ANY)
    merged, ortho, factor = pl.pallas_call(
        step_kernel,
        name="exchange",
        out_shape=(
            jax.ShapeDtypeStruct((BLKS, 128, BLK), BF16),
            jax.ShapeDtypeStruct((2, RANK, 128), BF16),
            jax.ShapeDtypeStruct((2, 2, 4, 4, 8, 16, 128), BF16),
        ),
        in_specs=[hbm] * 6,
        out_specs=(hbm, hbm, hbm),
        scratch_shapes=scratch,
        compiler_params=pltpu.CompilerParams(
            collective_id=0, has_side_effects=True, vmem_limit_bytes=40 * 2**20
        ),
    )(grad_key, error_key, prev_key.T, grad_val, error_val, prev_val.T)

    def rows(shape):
        return pl.BlockSpec(shape, lambda i: (0, i) if len(shape) == 2 else (0, 0, i))

    uk, nk, uv, nv, fk, fv = pl.pallas_call(
        out_kernel,
        name="outputs",
        grid=(8,),
        out_shape=(
            jax.ShapeDtypeStruct((ROWS, 8192), BF16), jax.ShapeDtypeStruct((1, ROWS, 8192), BF16),
            jax.ShapeDtypeStruct((ROWS, 8192), BF16), jax.ShapeDtypeStruct((1, ROWS, 8192), BF16),
            jax.ShapeDtypeStruct((RANK, BLK), F32), jax.ShapeDtypeStruct((RANK, BLK), F32),
        ),
        in_specs=[
            pl.BlockSpec((2, 128, BLK), lambda i: (i, 0, 0)),
            pl.BlockSpec((2, RANK, 128), lambda i: (0, 0, 0)),
            pl.BlockSpec((2, 1, 1, 4, 8, 16, 128), lambda i: (0, i // 4, i % 4, 0, 0, 0, 0)),
        ],
        out_specs=(
            rows((ROWS, 1024)), rows((1, ROWS, 1024)), rows((ROWS, 1024)), rows((1, ROWS, 1024)),
            pl.BlockSpec((RANK, BLK), lambda i: (0, 0)), pl.BlockSpec((RANK, BLK), lambda i: (0, 0)),
        ),
    )(merged, ortho, factor)
    return uk, nk, fk.T, uv, nv, fv.T


def solution(mesh):
    wide = P("replica", "shard", None)
    flat = P("shard", None)
    return jax.shard_map(
        per_device,
        mesh=mesh,
        in_specs=(wide, wide, flat, wide, wide, flat),
        out_specs=(flat, wide, flat, flat, wide, flat),
        check_vma=False,
    )
```

```python
import functools

import jax
import jax.numpy as jnp
from jax import lax
from jax.experimental import pallas as pl
from jax.experimental.pallas import tpu as pltpu
from jax.sharding import PartitionSpec as P

MESH = pl.DeviceIdType.MESH
F32, BF16 = jnp.float32, jnp.bfloat16
NX, NY, NZ, NC = 4, 4, 8, 2
REPLICAS = 16
RANK = 64
ROWS = 64
BLK = 512
BLKS = 16
COL = 256
COLS = 32
RIDGE = 1e-6
NT = (((1,), (1,)), ((), ()))
NN = (((1,), (0,)), ((), ()))


def device(x, y, z, c):
    return (lax.rem(y, 2) * NZ + z, (lax.div(y, 2) * NX + x) * NC + c)


def send(src, dst, ssem, rsem, dev):
    copy = pltpu.make_async_remote_copy(
        src_ref=src, dst_ref=dst, send_sem=ssem, recv_sem=rsem, device_id=dev, device_id_type=MESH
    )
    copy.start()
    return copy


def arrival(dst, ssem, rsem, dev):
    pltpu.make_async_remote_copy(
        src_ref=dst, dst_ref=dst, send_sem=ssem, recv_sem=rsem, device_id=dev, device_id_type=MESH
    ).wait_recv()


def lanes_low(shape):
    return lax.broadcasted_iota(jnp.int32, shape, 1) < RANK


def solve_rows(gram, left):
    shape = (RANK, 128)
    row = lax.broadcasted_iota(jnp.int32, shape, 0)
    lane = lax.broadcasted_iota(jnp.int32, shape, 1)
    low = lane < RANK
    swapped = pltpu.roll(left, RANK, 1)
    out = []
    for side in range(2):
        here = low if side == 0 else jnp.logical_not(low)
        diag = lane == row + side * RANK
        trace = jnp.sum(jnp.where(diag, gram, 0.0))
        ridge = RIDGE * (trace / RANK)
        whole = jnp.where(here, gram + jnp.where(diag, ridge, 0.0), swapped)
        out.append([whole[8 * t : 8 * t + 8] for t in range(8)])
    sub = lax.broadcasted_iota(jnp.int32, (8, 128), 0)
    for j in range(RANK - 1):
        top, pos = divmod(j, 8)
        for side in range(2):
            tiles = out[side]
            col = side * RANK + j
            pivot_row = tiles[top][pos : pos + 1, :]
            inv = 1.0 / pivot_row[:, col : col + 1]
            scaled = pivot_row * inv
            for t in range(top, 8):
                if t == top:
                    if pos == 7:
                        continue
                    factor = jnp.where(sub > pos, jnp.broadcast_to(tiles[t][:, col : col + 1], (8, 128)), 0.0)
                else:
                    factor = tiles[t][:, col : col + 1]
                tiles[t] = tiles[t] - factor * scaled
    done = []
    for side in range(2):
        whole = jnp.concatenate(out[side], axis=0)
        diag = lane == row + side * RANK
        pivots = jnp.sum(jnp.where(diag, whole, 0.0), axis=1, keepdims=True)
        done.append(pltpu.roll(whole * lax.rsqrt(pivots), RANK, 1))
    return jnp.where(low, done[0], 0.0), jnp.where(low, 0.0, done[1])


def step_kernel(
    gk, ek, pk, gv, ev, pv,
    uk, nk, fk, uv, nv, fv,
    grads, errors, mbuf, pbuf, acc, lbuf, r1, lt2, gp, cpair, c1, cfull, obl,
    obuf, wbuf, pr, s1, r2, s2, r3, s3, r4, fbuf, fstage,
    load_sem, out_sem, fac_sem,
    a_ss, a_rs, q_ss, q_rs, af_ss, af_rs, b_ss, b_rs, b2_ss, b2_rs, c0_ss, c0_rs, c1_ss, c1_rs, c2_ss, c2_rs,
    e0_ss, e0_rs, e1_ss, e1_rs, e2_ss, e2_rs, e3_ss, e3_rs,
    g3_ss, g3_rs, g2_ss, g2_rs, g1_ss, g1_rs, g0_ss, g0_rs,
):
    r = lax.axis_index("replica")
    s = lax.axis_index("shard")
    y_lo, z = lax.div(r, NZ), lax.rem(r, NZ)
    y_hi, x, c = lax.div(s, NX * NC), lax.rem(lax.div(s, NC), NX), lax.rem(s, NC)
    y = 2 * y_hi + y_lo
    oc = 1 - c
    cross = lax.rem(y + 3 + 2 * y_lo, NY)
    flip = 2 * y_hi + 1 - y_lo
    mate = device(x, y, z, oc)

    def at_x(d):
        return lax.rem(x + d, NX)

    def at_y(d):
        return lax.rem(y + d, NY)

    def at_z(d):
        return lax.rem(z + d, NZ)

    own_prev = [
        pltpu.make_async_copy(pk, pbuf.at[s, pl.ds(0, RANK)], load_sem.at[4]),
        pltpu.make_async_copy(pv, pbuf.at[s, pl.ds(RANK, RANK)], load_sem.at[5]),
    ]
    loads = [
        pltpu.make_async_copy(gk.at[0], grads.at[0], load_sem.at[0]),
        pltpu.make_async_copy(ek.at[0], errors.at[0], load_sem.at[1]),
        pltpu.make_async_copy(gv.at[0], grads.at[1], load_sem.at[2]),
        pltpu.make_async_copy(ev.at[0], errors.at[1], load_sem.at[3]),
    ]
    partners = [device(x, flip, at_z(d), c) for d in (4, 3, 5, 2, 6, 1, 7)]
    partners += [device(x, y, at_z(d), c) for d in (4, 3, 5, 2, 6, 1, 7)]
    partners += [device(at_x(d), cross, z, c) for d in (2, 1, 3)]
    partners += [device(at_x(d), y, z, c) for d in (2, 1, 3)]
    partners += [device(x, at_y(d), z, c) for d in (2, 1, 3)]
    partners += [mate]
    barrier = pltpu.get_barrier_semaphore()
    for dev in partners:
        pl.semaphore_signal(barrier, inc=1, device_id=dev, device_id_type=MESH)
    for copy in own_prev + loads:
        copy.start()
    for copy in own_prev:
        copy.wait()
    pl.semaphore_wait(barrier, len(partners))

    sent = []

    far = [(2, 1), (1, 1), (3, 1), (2, 0), (1, 0), (3, 0), (0, 1)]

    def quarter(slot, q):
        return pbuf.at[slot, pl.ds(pl.multiple_of(lax.rem(q, 4) * 32, 32), 32)]

    color = z + 2 * y_lo
    for i, (dx, over) in enumerate(far):
        dev = device(at_x(dx), cross if over else y, z, c)
        piece = quarter(s, color + 2 * over)
        sent.append(send(piece, piece, a_ss.at[i], a_rs.at[i], dev))
    sent.append(send(pbuf.at[s], pbuf.at[s], af_ss.at[7], af_rs.at[7], mate))
    near = (device(x, flip, z, c), device(x, y, at_z(1), c), device(x, y, at_z(7), c))

    for copy in loads:
        copy.wait()

    def merge(b, carry):
        cols = pl.ds(pl.multiple_of(b * COL, COL), COL)
        for m in range(2):
            total = grads[m, :, cols].astype(F32) + errors[m, :, cols].astype(F32)
            mbuf[b, m * ROWS : (m + 1) * ROWS, :] = total.astype(BF16)
        return carry

    lax.fori_loop(0, COLS, merge, 0)

    def left_term(slot):
        low = lax.dot_general(pbuf[slot, :, 0:COL], mbuf[2 * slot], NT, preferred_element_type=F32)
        high = lax.dot_general(pbuf[slot, :, COL:], mbuf[2 * slot + 1], NT, preferred_element_type=F32)
        return low + high

    acc[...] = left_term(s)
    order = (4, 5, 6, 1, 2, 3, 0)
    slots = []
    for i, (dx, over) in enumerate(far):
        yy = (1 - y_hi) if over else y_hi
        slots.append((yy * NX + lax.rem(x + NX - dx, NX)) * NC)
    for i in order:
        piece = quarter(slots[i] + c, color)
        arrival(piece, a_ss.at[i], a_rs.at[i], mate)
        for n in range(3):
            sent.append(send(piece, piece, q_ss.at[i, n], q_rs.at[i, n], near[n]))
    for i in order:
        slot = slots[i] + c
        for n in range(3):
            arrival(quarter(slot, color + (2, 3, 1)[n]), q_ss.at[i, n], q_rs.at[i, n], mate)
        sent.append(send(pbuf.at[slot], pbuf.at[slot], af_ss.at[i], af_rs.at[i], mate))
        acc[...] += left_term(slot)
    for i in (7,) + order:
        slot = (s + oc - c) if i == 7 else slots[i] + oc
        arrival(pbuf.at[slot], af_ss.at[i], af_rs.at[i], mate)
        acc[...] += left_term(slot)

    low64 = lanes_low((RANK, 128))
    part = jnp.where(low64, acc[0:RANK, :], acc[RANK:, :])
    for t in range(NZ):
        lbuf[t] = part[8 * t : 8 * t + 8]
    r1[r] = lbuf[z]
    peers = [(1, d) for d in (4, 3, 5, 2, 6, 1, 7, 0)] + [(0, d) for d in (4, 3, 5, 2, 6, 1, 7)]
    for i, (over, dz) in enumerate(peers):
        dev = device(x, flip if over else y, at_z(dz), c)
        sent.append(send(lbuf.at[at_z(dz)], r1.at[r], b_ss.at[i], b_rs.at[i], dev))
    for i, (over, dz) in enumerate(peers):
        slot = ((1 - y_lo) if over else y_lo) * NZ + lax.rem(z + NZ - dz, NZ)
        arrival(r1.at[slot], b_ss.at[i], b_rs.at[i], mate)
    total = r1[0]
    for t in range(1, REPLICAS):
        total = total + r1[t]
    lt2[z] = total / REPLICAS
    zs = (4, 3, 5, 2, 6, 1, 7)
    for i, dz in enumerate(zs):
        sent.append(send(lt2.at[z], lt2.at[z], b2_ss.at[i], b2_rs.at[i], device(x, y, at_z(dz), c)))
    for i, dz in enumerate(zs):
        arrival(lt2.at[lax.rem(z + NZ - dz, NZ)], b2_ss.at[i], b2_rs.at[i], mate)

    left = jnp.concatenate([lt2[t] for t in range(NZ)], axis=0)
    wide = jnp.concatenate([jnp.where(low64, left, 0.0), jnp.where(low64, 0.0, left)], axis=0)
    gram = lax.dot_general(wide, wide, NT, precision=lax.Precision.HIGHEST, preferred_element_type=F32)
    gram = jnp.where(low64, gram[0:RANK], gram[RANK:])
    gp[0] = gram[0:32]
    gp[1] = gram[32:64]
    copy = send(gp.at[oc], cpair, c0_ss, c0_rs, mate)
    copy.wait_recv()
    sent.append(copy)
    chip = y_hi * NX + x
    c1[chip] = gp[c] + cpair[...]
    for i, (dx, over) in enumerate(far):
        dev = device(at_x(dx), cross if over else y, z, c)
        sent.append(send(c1.at[chip], c1.at[chip], c1_ss.at[i], c1_rs.at[i], dev))
    for i, (dx, over) in enumerate(far):
        arrival(c1.at[lax.div(slots[i], NC)], c1_ss.at[i], c1_rs.at[i], mate)
    total = c1[0]
    for t in range(1, 8):
        total = total + c1[t]
    cfull[c] = total
    copy = send(cfull.at[c], cfull.at[c], c2_ss, c2_rs, mate)
    arrival(cfull.at[oc], c2_ss, c2_rs, mate)
    sent.append(copy)
    gram = jnp.concatenate([cfull[0], cfull[1]], axis=0)

    key_rows, val_rows = solve_rows(gram, left)
    obl[0] = key_rows
    obl[1] = val_rows

    ordered = jnp.concatenate([obl[oc], obl[c]], axis=0).astype(BF16)
    firsts = (x, y)
    seconds = (y, x)
    ds = (2, 1, 3, 0)

    def first(pq, d):
        return lax.rem(firsts[pq] + d, 4)

    def second(pq, d):
        return lax.rem(seconds[pq] + d, 4)

    def dev1(pq, d):
        return device(at_x(d), y, z, c) if pq == 0 else device(x, at_y(d), z, c)

    def dev2(pq, d):
        return device(x, at_y(d), z, c) if pq == 0 else device(at_x(d), y, z, c)

    pair_copies = {}
    for j, dj in enumerate(ds):
        for pq in range(2):
            i2 = second(pq, dj)
            for i1 in range(4):
                term = lax.dot_general(ordered, mbuf[pq * 16 + i1 * 4 + i2], NN, preferred_element_type=F32)
                for a in range(4):
                    for b in range(2):
                        cols = slice(b * 128, b * 128 + 128)
                        obuf[pq, i2, i1, 2 * a + b] = term[16 * a : 16 * a + 16, cols].astype(BF16)
                        wbuf[pq, i2, i1, 2 * a + b] = term[64 + 16 * a : 80 + 16 * a, cols]
            pair_copies[pq, j] = send(
                obuf.at[pq, i2], pr.at[pq, i2], e0_ss.at[pq, j], e0_rs.at[pq, j], mate
            )
    for j, dj in enumerate(ds):
        for pq in range(2):
            i2 = second(pq, dj)
            pair_copies[pq, j].wait_recv()
            sent.append(pair_copies[pq, j])
            for k, dk in enumerate(ds):
                i1 = first(pq, dk)
                total = wbuf[pq, i2, i1] + pr[pq, i2, i1].astype(F32)
                if dk == 0:
                    wbuf[pq, i2, i1] = total
                else:
                    s1[pq, j, k] = total.astype(BF16)
                    sent.append(
                        send(s1.at[pq, j, k], r2.at[pq, j, k], e1_ss.at[pq, j, k], e1_rs.at[pq, j, k], dev1(pq, dk))
                    )
    for j, dj in enumerate(ds):
        for pq in range(2):
            i1, i2 = first(pq, 0), second(pq, dj)
            total = wbuf[pq, i2, i1]
            for k in range(3):
                arrival(r2.at[pq, j, k], e1_ss.at[pq, j, k], e1_rs.at[pq, j, k], mate)
                total = total + r2[pq, j, k].astype(F32)
            if dj == 0:
                wbuf[pq, i2, i1] = total
            else:
                s2[pq, j] = total.astype(BF16)
                sent.append(
                    send(s2.at[pq, j], r3.at[pq, j], e2_ss.at[pq, j], e2_rs.at[pq, j], dev2(pq, dj))
                )
    for pq in range(2):
        i1, i2 = first(pq, 0), second(pq, 0)
        total = wbuf[pq, i2, i1]
        for j in range(3):
            arrival(r3.at[pq, j], e2_ss.at[pq, j], e2_rs.at[pq, j], mate)
            total = total + r3[pq, j].astype(F32)
        wbuf[pq, i2, i1] = total
        s3[:, pq] = total.astype(BF16)
    for i, dz in enumerate(zs):
        there = at_z(dz)
        sent.append(send(s3.at[there], r4.at[i], e3_ss.at[i], e3_rs.at[i], device(x, y, there, c)))
    for i in range(7):
        arrival(r4.at[i], e3_ss.at[i], e3_rs.at[i], mate)
    for pq in range(2):
        i1, i2 = first(pq, 0), second(pq, 0)
        total = wbuf[pq, i2, i1, z]
        for i in range(7):
            total = total + r4[i, pq].astype(F32)
        fbuf[c, pq, i1, i2, z] = (total / REPLICAS).astype(BF16)

    for pq in range(2):
        piece = fbuf.at[c, pq, first(pq, 0), second(pq, 0), z]
        for i, dz in enumerate(zs):
            sent.append(send(piece, piece, g3_ss.at[pq, i], g3_rs.at[pq, i], device(x, y, at_z(dz), c)))
    ortho = jnp.concatenate([obl[0], obl[1]], axis=0).T.astype(BF16)

    def sub_piece(pq, k, j):
        return fbuf.at[c, pq, first(pq, 4 - ds[k]), second(pq, 4 - ds[j])]

    def spread(pq, j):
        piece = sub_piece(pq, 3, j)
        for k in range(3):
            sent.append(send(piece, piece, g1_ss.at[pq, j, k], g1_rs.at[pq, j, k], dev1(pq, ds[k])))

    for pq in range(2):
        piece = sub_piece(pq, 3, 3)
        for i, dz in enumerate(zs):
            arrival(
                fbuf.at[c, pq, first(pq, 0), second(pq, 0), lax.rem(z + NZ - dz, NZ)],
                g3_ss.at[pq, i], g3_rs.at[pq, i], mate,
            )
        for k in range(3):
            sent.append(send(piece, piece, g2_ss.at[pq, k], g2_rs.at[pq, k], dev2(pq, ds[k])))
        spread(pq, 3)
    for j in (1, 2, 0):
        for pq in range(2):
            arrival(sub_piece(pq, 3, j), g2_ss.at[pq, j], g2_rs.at[pq, j], mate)
            spread(pq, j)

    stores = []

    def finish(n, pq, k):
        i1 = first(pq, 4 - ds[k])
        arrival(fbuf.at[oc, pq, i1], g0_ss.at[pq, k], g0_rs.at[pq, k], mate)
        at = pl.multiple_of(pq * 4096 + i1 * 1024, 1024)
        for i in range(4):
            sides = []
            for m in range(2):
                rows = [
                    jnp.concatenate([fbuf[m, pq, i1, i, 2 * a], fbuf[m, pq, i1, i, 2 * a + 1]], axis=1)
                    for a in range(4)
                ]
                sides.append(jnp.concatenate(rows, axis=0))
            factor = jnp.concatenate(sides, axis=0)
            approx = lax.dot_general(ortho, factor, NN, preferred_element_type=F32)
            rest = (mbuf[pq * 16 + i1 * 4 + i].astype(F32) - approx).astype(BF16)
            approx = approx.astype(BF16)
            cols = pl.ds(pl.multiple_of(at + i * COL, COL), COL)
            for m in range(2):
                grads[m, :, cols] = approx[m * ROWS : m * ROWS + ROWS]
                errors[m, :, cols] = rest[m * ROWS : m * ROWS + ROWS]
        cols = pl.ds(at, 1024)
        for i, (src, dst) in enumerate(
            (
                (grads.at[0, :, cols], uk.at[:, cols]),
                (errors.at[0, :, cols], nk.at[0, :, cols]),
                (grads.at[1, :, cols], uv.at[:, cols]),
                (errors.at[1, :, cols], nv.at[0, :, cols]),
            )
        ):
            copy = pltpu.make_async_copy(src, dst, out_sem.at[n, i])
            copy.start()
            stores.append(copy)

    pending = None
    for k in (3, 1, 2, 0):
        for pq in range(2):
            if k < 3:
                for j in (3, 1, 2, 0):
                    arrival(sub_piece(pq, k, j), g1_ss.at[pq, j, k], g1_rs.at[pq, j, k], mate)
            piece = fbuf.at[c, pq, first(pq, 4 - ds[k])]
            sent.append(send(piece, piece, g0_ss.at[pq, k], g0_rs.at[pq, k], mate))
            if pending is not None:
                finish(*pending)
            pending = (2 * k + pq, pq, k)
    finish(*pending)
    for i in range(2):
        for m in range(2):
            rows = [
                jnp.concatenate([fbuf[m, s // 8, s % 8 // 2, s % 2 * 2 + i, 2 * a + b] for b in range(2)], axis=1)
                for a in range(4)
            ]
            fstage[m, :, i * COL : (i + 1) * COL] = jnp.concatenate(rows, axis=0).astype(F32)
    for m, dst in enumerate((fk, fv)):
        copy = pltpu.make_async_copy(fstage.at[m], dst, fac_sem.at[m])
        copy.start()
        stores.append(copy)
    for copy in stores:
        copy.wait()
    for copy in sent:
        copy.wait_send()


def per_device(grad_key, error_key, prev_key, grad_val, error_val, prev_val):
    vm = pltpu.VMEM
    dma = pltpu.SemaphoreType.DMA
    scratch = [
        vm((2, ROWS, 8192), BF16), vm((2, ROWS, 8192), BF16),
        vm((COLS, 128, COL), BF16), vm((BLKS, 128, BLK), BF16),
        vm((128, 128), F32), vm((8, 8, 128), F32), vm((16, 8, 128), F32), vm((8, 8, 128), F32),
        vm((2, 32, 128), F32), vm((32, 128), F32), vm((8, 32, 128), F32), vm((2, 32, 128), F32),
        vm((2, RANK, 128), F32),
        vm((2, 4, 4, 8, 16, 128), BF16), vm((2, 4, 4, 8, 16, 128), F32), vm((2, 4, 4, 8, 16, 128), BF16),
        vm((2, 4, 3, 8, 16, 128), BF16), vm((2, 4, 3, 8, 16, 128), BF16),
        vm((2, 3, 8, 16, 128), BF16), vm((2, 3, 8, 16, 128), BF16),
        vm((8, 2, 16, 128), BF16), vm((7, 2, 16, 128), BF16),
        vm((2, 2, 4, 4, 8, 16, 128), BF16), vm((2, RANK, BLK), F32),
        dma((6,)), dma((8, 4)), dma((2,)),
    ]
    for n in (
        (7,), (7, 3), (8,), (15,), (7,), None, (7,), None,
        (2, 4), (2, 4, 3), (2, 3), (7,), (2, 7), (2, 3), (2, 4, 3), (2, 4),
    ):
        for _ in range(2):
            scratch.append(dma if n is None else dma(n))
    hbm = pl.BlockSpec(memory_space=pl.ANY)
    out = pl.BlockSpec(memory_space=pl.ANY)
    update = jax.ShapeDtypeStruct((ROWS, 8192), BF16)
    rest = jax.ShapeDtypeStruct((1, ROWS, 8192), BF16)
    factor = jax.ShapeDtypeStruct((RANK, BLK), F32)
    uk, nk, fk, uv, nv, fv = pl.pallas_call(
        step_kernel,
        name="exchange",
        out_shape=(update, rest, factor, update, rest, factor),
        in_specs=[hbm] * 6,
        out_specs=(out,) * 6,
        scratch_shapes=scratch,
        compiler_params=pltpu.CompilerParams(
            collective_id=0, has_side_effects=True, vmem_limit_bytes=60 * 2**20
        ),
    )(grad_key, error_key, prev_key.T, grad_val, error_val, prev_val.T)
    return uk, nk, fk.T, uv, nv, fv.T


def solution(mesh):
    wide = P("replica", "shard", None)
    flat = P("shard", None)
    return jax.shard_map(
        per_device,
        mesh=mesh,
        in_specs=(wide, wide, flat, wide, wide, flat),
        out_specs=(flat, wide, flat, flat, wide, flat),
        check_vma=False,
    )
```

```python
import functools

import jax
import jax.numpy as jnp
from jax import lax
from jax.experimental import pallas as pl
from jax.experimental.pallas import tpu as pltpu
from jax.sharding import PartitionSpec as P

MESH = pl.DeviceIdType.MESH
F32, BF16 = jnp.float32, jnp.bfloat16
NX, NY, NZ, NC = 4, 4, 8, 2
REPLICAS = 16
RANK = 64
ROWS = 64
BLK = 512
BLKS = 16
COL = 256
COLS = 32
RIDGE = 1e-6
NT = (((1,), (1,)), ((), ()))
NN = (((1,), (0,)), ((), ()))


def device(x, y, z, c):
    return (lax.rem(y, 2) * NZ + z, (lax.div(y, 2) * NX + x) * NC + c)


def send(src, dst, ssem, rsem, dev):
    copy = pltpu.make_async_remote_copy(
        src_ref=src, dst_ref=dst, send_sem=ssem, recv_sem=rsem, device_id=dev, device_id_type=MESH
    )
    copy.start()
    return copy


def arrival(dst, ssem, rsem, dev):
    pltpu.make_async_remote_copy(
        src_ref=dst, dst_ref=dst, send_sem=ssem, recv_sem=rsem, device_id=dev, device_id_type=MESH
    ).wait_recv()


def lanes_low(shape):
    return lax.broadcasted_iota(jnp.int32, shape, 1) < RANK


def solve_rows(gram, left):
    shape = (RANK, 128)
    row = lax.broadcasted_iota(jnp.int32, shape, 0)
    lane = lax.broadcasted_iota(jnp.int32, shape, 1)
    low = lane < RANK
    swapped = pltpu.roll(left, RANK, 1)
    rest = []
    for side in range(2):
        here = low if side == 0 else jnp.logical_not(low)
        diag = lane == row + side * RANK
        trace = jnp.sum(jnp.where(diag, gram, 0.0))
        ridge = RIDGE * (trace / RANK)
        rest.append(jnp.where(here, gram + jnp.where(diag, ridge, 0.0), swapped))
    sub = lax.broadcasted_iota(jnp.int32, (8, 128), 0)
    done = [[], []]
    for t in range(8):
        count = RANK - 8 * t
        head = [rest[side][:8] for side in range(2)]
        tail = [rest[side][8:] if t < 7 else None for side in range(2)]
        hcol, tcol = [], []
        for side in range(2):
            first = side * RANK + 8 * t
            cols = [jnp.broadcast_to(rest[side][:, first + k : first + k + 1], (count, 128)) for k in range(8)]
            hcol.append([col[:8] for col in cols])
            tcol.append([col[8:] for col in cols] if t < 7 else None)
        for k in range(8):
            for side in range(2):
                inv = 1.0 / hcol[side][k][k : k + 1, :]
                across = [hcol[side][j][k : k + 1, :] for j in range(8)]
                pivot = head[side][k : k + 1, :]
                if k < 7:
                    m = jnp.where(sub > k, hcol[side][k] * inv, 0.0)
                    for j in range(k + 1, 8):
                        hcol[side][j] = hcol[side][j] - m * across[j]
                    head[side] = head[side] - m * pivot
                if t < 7:
                    m = tcol[side][k] * inv
                    for j in range(k + 1, 8):
                        tcol[side][j] = tcol[side][j] - m * across[j]
                    tail[side] = tail[side] - m * pivot
        for side in range(2):
            done[side].append(head[side])
        rest = tail
    out = []
    for side in range(2):
        whole = jnp.concatenate(done[side], axis=0)
        diag = lane == row + side * RANK
        pivots = jnp.sum(jnp.where(diag, whole, 0.0), axis=1, keepdims=True)
        out.append(pltpu.roll(whole * lax.rsqrt(pivots), RANK, 1))
    return jnp.where(low, out[0], 0.0), jnp.where(low, 0.0, out[1])


def step_kernel(
    gk, ek, pk, gv, ev, pv,
    uk, nk, fk, uv, nv, fv,
    grads, errors, mbuf, pbuf, acc, lbuf, r1, lt2, gp, cpair, c1, cfull, obl,
    obuf, wbuf, pr, s1, r2, s2, r3, s3, r4, fbuf, fstage,
    load_sem, out_sem, fac_sem,
    a_ss, a_rs, q_ss, q_rs, af_ss, af_rs, b_ss, b_rs, b2_ss, b2_rs, c0_ss, c0_rs, c1_ss, c1_rs, c2_ss, c2_rs,
    e0_ss, e0_rs, e1_ss, e1_rs, e2_ss, e2_rs, e3_ss, e3_rs,
    g3_ss, g3_rs, g2_ss, g2_rs, g1_ss, g1_rs, g0_ss, g0_rs,
):
    r = lax.axis_index("replica")
    s = lax.axis_index("shard")
    y_lo, z = lax.div(r, NZ), lax.rem(r, NZ)
    y_hi, x, c = lax.div(s, NX * NC), lax.rem(lax.div(s, NC), NX), lax.rem(s, NC)
    y = 2 * y_hi + y_lo
    oc = 1 - c
    cross = lax.rem(y + 3 + 2 * y_lo, NY)
    flip = 2 * y_hi + 1 - y_lo
    mate = device(x, y, z, oc)

    def at_x(d):
        return lax.rem(x + d, NX)

    def at_y(d):
        return lax.rem(y + d, NY)

    def at_z(d):
        return lax.rem(z + d, NZ)

    own_prev = [
        pltpu.make_async_copy(pk, pbuf.at[s, pl.ds(0, RANK)], load_sem.at[4]),
        pltpu.make_async_copy(pv, pbuf.at[s, pl.ds(RANK, RANK)], load_sem.at[5]),
    ]
    loads = [
        pltpu.make_async_copy(gk.at[0], grads.at[0], load_sem.at[0]),
        pltpu.make_async_copy(ek.at[0], errors.at[0], load_sem.at[1]),
        pltpu.make_async_copy(gv.at[0], grads.at[1], load_sem.at[2]),
        pltpu.make_async_copy(ev.at[0], errors.at[1], load_sem.at[3]),
    ]
    partners = [device(x, flip, at_z(d), c) for d in (4, 3, 5, 2, 6, 1, 7)]
    partners += [device(x, y, at_z(d), c) for d in (4, 3, 5, 2, 6, 1, 7)]
    partners += [device(at_x(d), cross, z, c) for d in (2, 1, 3)]
    partners += [device(at_x(d), y, z, c) for d in (2, 1, 3)]
    partners += [device(x, at_y(d), z, c) for d in (2, 1, 3)]
    partners += [mate]
    barrier = pltpu.get_barrier_semaphore()
    for dev in partners:
        pl.semaphore_signal(barrier, inc=1, device_id=dev, device_id_type=MESH)
    for copy in own_prev + loads:
        copy.start()
    for copy in own_prev:
        copy.wait()
    pl.semaphore_wait(barrier, len(partners))

    sent = []

    def take():
        old = sent[:]
        sent.clear()
        return old

    def settle(copies):
        for copy in copies:
            copy.wait_send()

    far = [(2, 1), (1, 1), (3, 1), (2, 0), (1, 0), (3, 0), (0, 1)]

    def quarter(slot, q):
        return pbuf.at[slot, pl.ds(pl.multiple_of(lax.rem(q, 4) * 32, 32), 32)]

    color = z + 2 * y_lo
    for i, (dx, over) in enumerate(far):
        dev = device(at_x(dx), cross if over else y, z, c)
        piece = quarter(s, color + 2 * over)
        sent.append(send(piece, piece, a_ss.at[i], a_rs.at[i], dev))
    sent.append(send(pbuf.at[s], pbuf.at[s], af_ss.at[7], af_rs.at[7], mate))
    near = (device(x, flip, z, c), device(x, y, at_z(1), c), device(x, y, at_z(7), c))

    for copy in loads:
        copy.wait()

    def merge(b, carry):
        cols = pl.ds(pl.multiple_of(b * COL, COL), COL)
        for m in range(2):
            total = grads[m, :, cols].astype(F32) + errors[m, :, cols].astype(F32)
            mbuf[b, m * ROWS : (m + 1) * ROWS, :] = total.astype(BF16)
        return carry

    lax.fori_loop(0, COLS, merge, 0)

    def left_term(slot):
        low = lax.dot_general(pbuf[slot, :, 0:COL], mbuf[2 * slot], NT, preferred_element_type=F32)
        high = lax.dot_general(pbuf[slot, :, COL:], mbuf[2 * slot + 1], NT, preferred_element_type=F32)
        return low + high

    acc[...] = left_term(s)
    order = (4, 5, 6, 1, 2, 3, 0)
    slots = []
    for i, (dx, over) in enumerate(far):
        yy = (1 - y_hi) if over else y_hi
        slots.append((yy * NX + lax.rem(x + NX - dx, NX)) * NC)
    for i in order:
        piece = quarter(slots[i] + c, color)
        arrival(piece, a_ss.at[i], a_rs.at[i], mate)
        for n in range(3):
            sent.append(send(piece, piece, q_ss.at[i, n], q_rs.at[i, n], near[n]))
    for i in order:
        slot = slots[i] + c
        for n in range(3):
            arrival(quarter(slot, color + (2, 3, 1)[n]), q_ss.at[i, n], q_rs.at[i, n], mate)
        sent.append(send(pbuf.at[slot], pbuf.at[slot], af_ss.at[i], af_rs.at[i], mate))
        acc[...] += left_term(slot)
    for i in (7,) + order:
        slot = (s + oc - c) if i == 7 else slots[i] + oc
        arrival(pbuf.at[slot], af_ss.at[i], af_rs.at[i], mate)
        acc[...] += left_term(slot)

    low64 = lanes_low((RANK, 128))
    part = jnp.where(low64, acc[0:RANK, :], acc[RANK:, :])
    for t in range(NZ):
        lbuf[t] = part[8 * t : 8 * t + 8]
    r1[r] = lbuf[z]
    old = take()
    peers = [(1, d) for d in (4, 3, 5, 2, 6, 1, 7, 0)] + [(0, d) for d in (4, 3, 5, 2, 6, 1, 7)]
    for i, (over, dz) in enumerate(peers):
        dev = device(x, flip if over else y, at_z(dz), c)
        sent.append(send(lbuf.at[at_z(dz)], r1.at[r], b_ss.at[i], b_rs.at[i], dev))
    settle(old)
    for i, (over, dz) in enumerate(peers):
        slot = ((1 - y_lo) if over else y_lo) * NZ + lax.rem(z + NZ - dz, NZ)
        arrival(r1.at[slot], b_ss.at[i], b_rs.at[i], mate)
    total = r1[0]
    for t in range(1, REPLICAS):
        total = total + r1[t]
    lt2[z] = total / REPLICAS
    zs = (4, 3, 5, 2, 6, 1, 7)
    old = take()
    for i, dz in enumerate(zs):
        sent.append(send(lt2.at[z], lt2.at[z], b2_ss.at[i], b2_rs.at[i], device(x, y, at_z(dz), c)))
    settle(old)
    for i, dz in enumerate(zs):
        arrival(lt2.at[lax.rem(z + NZ - dz, NZ)], b2_ss.at[i], b2_rs.at[i], mate)

    left = jnp.concatenate([lt2[t] for t in range(NZ)], axis=0)
    wide = jnp.concatenate([jnp.where(low64, left, 0.0), jnp.where(low64, 0.0, left)], axis=0)
    gram = lax.dot_general(wide, wide, NT, precision=lax.Precision.HIGHEST, preferred_element_type=F32)
    gram = jnp.where(low64, gram[0:RANK], gram[RANK:])
    gp[0] = gram[0:32]
    gp[1] = gram[32:64]
    copy = send(gp.at[oc], cpair, c0_ss, c0_rs, mate)
    copy.wait_recv()
    sent.append(copy)
    chip = y_hi * NX + x
    c1[chip] = gp[c] + cpair[...]
    old = take()
    for i, (dx, over) in enumerate(far):
        dev = device(at_x(dx), cross if over else y, z, c)
        sent.append(send(c1.at[chip], c1.at[chip], c1_ss.at[i], c1_rs.at[i], dev))
    settle(old)
    for i, (dx, over) in enumerate(far):
        arrival(c1.at[lax.div(slots[i], NC)], c1_ss.at[i], c1_rs.at[i], mate)
    total = c1[0]
    for t in range(1, 8):
        total = total + c1[t]
    cfull[c] = total
    copy = send(cfull.at[c], cfull.at[c], c2_ss, c2_rs, mate)
    arrival(cfull.at[oc], c2_ss, c2_rs, mate)
    sent.append(copy)
    gram = jnp.concatenate([cfull[0], cfull[1]], axis=0)

    key_rows, val_rows = solve_rows(gram, left)
    obl[0] = key_rows
    obl[1] = val_rows

    ordered = jnp.concatenate([obl[oc], obl[c]], axis=0).astype(BF16)
    firsts = (x, y)
    seconds = (y, x)
    ds = (2, 1, 3, 0)

    def first(pq, d):
        return lax.rem(firsts[pq] + d, 4)

    def second(pq, d):
        return lax.rem(seconds[pq] + d, 4)

    def dev1(pq, d):
        return device(at_x(d), y, z, c) if pq == 0 else device(x, at_y(d), z, c)

    def dev2(pq, d):
        return device(x, at_y(d), z, c) if pq == 0 else device(at_x(d), y, z, c)

    pair_copies = {}
    old = take()
    for j, dj in enumerate(ds):
        for pq in range(2):
            i2 = second(pq, dj)
            for i1 in range(4):
                term = lax.dot_general(ordered, mbuf[pq * 16 + i1 * 4 + i2], NN, preferred_element_type=F32)
                for a in range(4):
                    for b in range(2):
                        cols = slice(b * 128, b * 128 + 128)
                        obuf[pq, i2, i1, 2 * a + b] = term[16 * a : 16 * a + 16, cols].astype(BF16)
                        wbuf[pq, i2, i1, 2 * a + b] = term[64 + 16 * a : 80 + 16 * a, cols]
            pair_copies[pq, j] = send(
                obuf.at[pq, i2], pr.at[pq, i2], e0_ss.at[pq, j], e0_rs.at[pq, j], mate
            )
    settle(old)
    for j, dj in enumerate(ds):
        for pq in range(2):
            i2 = second(pq, dj)
            pair_copies[pq, j].wait_recv()
            for k, dk in enumerate(ds):
                i1 = first(pq, dk)
                total = wbuf[pq, i2, i1] + pr[pq, i2, i1].astype(F32)
                if dk == 0:
                    wbuf[pq, i2, i1] = total
                else:
                    s1[pq, j, k] = total.astype(BF16)
                    sent.append(
                        send(s1.at[pq, j, k], r2.at[pq, j, k], e1_ss.at[pq, j, k], e1_rs.at[pq, j, k], dev1(pq, dk))
                    )
    settle(copy for copy in pair_copies.values())
    for j, dj in enumerate(ds):
        for pq in range(2):
            i1, i2 = first(pq, 0), second(pq, dj)
            total = wbuf[pq, i2, i1]
            for k in range(3):
                arrival(r2.at[pq, j, k], e1_ss.at[pq, j, k], e1_rs.at[pq, j, k], mate)
                total = total + r2[pq, j, k].astype(F32)
            if dj == 0:
                wbuf[pq, i2, i1] = total
            else:
                s2[pq, j] = total.astype(BF16)
                sent.append(
                    send(s2.at[pq, j], r3.at[pq, j], e2_ss.at[pq, j], e2_rs.at[pq, j], dev2(pq, dj))
                )
    settle(take())
    for pq in range(2):
        i1, i2 = first(pq, 0), second(pq, 0)
        total = wbuf[pq, i2, i1]
        for j in range(3):
            arrival(r3.at[pq, j], e2_ss.at[pq, j], e2_rs.at[pq, j], mate)
            total = total + r3[pq, j].astype(F32)
        wbuf[pq, i2, i1] = total
        s3[:, pq] = total.astype(BF16)
    old = take()
    for i, dz in enumerate(zs):
        there = at_z(dz)
        sent.append(send(s3.at[there], r4.at[i], e3_ss.at[i], e3_rs.at[i], device(x, y, there, c)))
    settle(old)
    last = take()
    for i in range(7):
        arrival(r4.at[i], e3_ss.at[i], e3_rs.at[i], mate)
    for pq in range(2):
        i1, i2 = first(pq, 0), second(pq, 0)
        total = wbuf[pq, i2, i1, z]
        for i in range(7):
            total = total + r4[i, pq].astype(F32)
        fbuf[c, pq, i1, i2, z] = (total / REPLICAS).astype(BF16)

    for pq in range(2):
        piece = fbuf.at[c, pq, first(pq, 0), second(pq, 0), z]
        for i, dz in enumerate(zs):
            sent.append(send(piece, piece, g3_ss.at[pq, i], g3_rs.at[pq, i], device(x, y, at_z(dz), c)))
    settle(last)
    last = take()
    ortho = jnp.concatenate([obl[0], obl[1]], axis=0).T.astype(BF16)

    def sub_piece(pq, k, j):
        return fbuf.at[c, pq, first(pq, 4 - ds[k]), second(pq, 4 - ds[j])]

    def spread(pq, j):
        piece = sub_piece(pq, 3, j)
        for k in range(3):
            sent.append(send(piece, piece, g1_ss.at[pq, j, k], g1_rs.at[pq, j, k], dev1(pq, ds[k])))

    for pq in range(2):
        piece = sub_piece(pq, 3, 3)
        for i, dz in enumerate(zs):
            arrival(
                fbuf.at[c, pq, first(pq, 0), second(pq, 0), lax.rem(z + NZ - dz, NZ)],
                g3_ss.at[pq, i], g3_rs.at[pq, i], mate,
            )
        for k in range(3):
            sent.append(send(piece, piece, g2_ss.at[pq, k], g2_rs.at[pq, k], dev2(pq, ds[k])))
        spread(pq, 3)
    settle(last)
    for j in (1, 2, 0):
        for pq in range(2):
            arrival(sub_piece(pq, 3, j), g2_ss.at[pq, j], g2_rs.at[pq, j], mate)
            spread(pq, j)

    old = take()
    settle(old[:6])
    stores = []

    def finish(n, pq, k):
        i1 = first(pq, 4 - ds[k])
        arrival(fbuf.at[oc, pq, i1], g0_ss.at[pq, k], g0_rs.at[pq, k], mate)
        at = pl.multiple_of(pq * 4096 + i1 * 1024, 1024)
        for i in range(4):
            sides = []
            for m in range(2):
                rows = [
                    jnp.concatenate([fbuf[m, pq, i1, i, 2 * a], fbuf[m, pq, i1, i, 2 * a + 1]], axis=1)
                    for a in range(4)
                ]
                sides.append(jnp.concatenate(rows, axis=0))
            factor = jnp.concatenate(sides, axis=0)
            approx = lax.dot_general(ortho, factor, NN, preferred_element_type=F32)
            rest = (mbuf[pq * 16 + i1 * 4 + i].astype(F32) - approx).astype(BF16)
            approx = approx.astype(BF16)
            cols = pl.ds(pl.multiple_of(at + i * COL, COL), COL)
            for m, (u, e) in enumerate(((uk, nk), (uv, nv))):
                u[:, cols] = approx[m * ROWS : m * ROWS + ROWS]
                e[0, :, cols] = rest[m * ROWS : m * ROWS + ROWS]

    pending = None
    for k in (3, 1, 2, 0):
        for pq in range(2):
            if k < 3:
                for j in (3, 1, 2, 0):
                    arrival(sub_piece(pq, k, j), g1_ss.at[pq, j, k], g1_rs.at[pq, j, k], mate)
            piece = fbuf.at[c, pq, first(pq, 4 - ds[k])]
            sent.append(send(piece, piece, g0_ss.at[pq, k], g0_rs.at[pq, k], mate))
            if k == 0 and pq == 1:
                settle(old[6:])
            if pending is not None:
                finish(*pending)
            pending = (2 * k + pq, pq, k)
    finish(*pending)
    for i in range(2):
        for m in range(2):
            rows = [
                jnp.concatenate([fbuf[m, s // 8, s % 8 // 2, s % 2 * 2 + i, 2 * a + b] for b in range(2)], axis=1)
                for a in range(4)
            ]
            (fk, fv)[m][:, i * COL : (i + 1) * COL] = jnp.concatenate(rows, axis=0).astype(F32)
    for copy in stores:
        copy.wait()
    for copy in sent:
        copy.wait_send()


def flush_kernel(uk, nk, fk, uv, nv, fv, uk_out, nk_out, fk_out, uv_out, nv_out, fv_out, sems):
    pairs = [(fk, fk_out), (fv, fv_out)]
    for q in range(4):
        rows = pl.ds(16 * q, 16)
        pairs += [(uk.at[rows], uk_out.at[rows]), (uv.at[rows], uv_out.at[rows])]
        pairs += [(nk.at[0, rows], nk_out.at[0, rows]), (nv.at[0, rows], nv_out.at[0, rows])]
    copies = [pltpu.make_async_copy(src, dst, sems.at[i]) for i, (src, dst) in enumerate(pairs)]
    for copy in copies:
        copy.start()
    for copy in copies:
        copy.wait()


def per_device(grad_key, error_key, prev_key, grad_val, error_val, prev_val):
    vm = pltpu.VMEM
    dma = pltpu.SemaphoreType.DMA
    scratch = [
        vm((2, ROWS, 8192), BF16), vm((2, ROWS, 8192), BF16),
        vm((COLS, 128, COL), BF16), vm((BLKS, 128, BLK), BF16),
        vm((128, 128), F32), vm((8, 8, 128), F32), vm((16, 8, 128), F32), vm((8, 8, 128), F32),
        vm((2, 32, 128), F32), vm((32, 128), F32), vm((8, 32, 128), F32), vm((2, 32, 128), F32),
        vm((2, RANK, 128), F32),
        vm((2, 4, 4, 8, 16, 128), BF16), vm((2, 4, 4, 8, 16, 128), F32), vm((2, 4, 4, 8, 16, 128), BF16),
        vm((2, 4, 3, 8, 16, 128), BF16), vm((2, 4, 3, 8, 16, 128), BF16),
        vm((2, 3, 8, 16, 128), BF16), vm((2, 3, 8, 16, 128), BF16),
        vm((8, 2, 16, 128), BF16), vm((7, 2, 16, 128), BF16),
        vm((2, 2, 4, 4, 8, 16, 128), BF16), vm((2, RANK, BLK), F32),
        dma((6,)), dma((8, 4)), dma((2,)),
    ]
    for n in (
        (7,), (7, 3), (8,), (15,), (7,), None, (7,), None,
        (2, 4), (2, 4, 3), (2, 3), (7,), (2, 7), (2, 3), (2, 4, 3), (2, 4),
    ):
        for _ in range(2):
            scratch.append(dma if n is None else dma(n))
    hbm = pl.BlockSpec(memory_space=pl.ANY)
    out = pl.BlockSpec(memory_space=pltpu.VMEM)
    shapes = [((ROWS, 8192), BF16), ((1, ROWS, 8192), BF16), ((RANK, BLK), F32)] * 2
    operands = (grad_key, error_key, prev_key.T, grad_val, error_val, prev_val.T)
    held = pl.pallas_call(
        step_kernel,
        name="exchange",
        out_shape=tuple(pltpu.VMEM(*one) for one in shapes),
        in_specs=[hbm] * 6,
        out_specs=(out,) * 6,
        scratch_shapes=scratch,
        compiler_params=pltpu.CompilerParams(
            collective_id=0, has_side_effects=True, vmem_limit_bytes=32 * 2**20
        ),
    )(*(pltpu.with_memory_space_constraint(one, pltpu.HBM) for one in operands))
    uk, nk, fk, uv, nv, fv = pl.pallas_call(
        flush_kernel,
        name="flush",
        out_shape=tuple(jax.ShapeDtypeStruct(*one) for one in shapes),
        in_specs=[pl.BlockSpec(memory_space=pltpu.VMEM)] * 6,
        out_specs=(hbm,) * 6,
        scratch_shapes=[dma((20,))],
        compiler_params=pltpu.CompilerParams(vmem_limit_bytes=2**21),
    )(*(pltpu.with_memory_space_constraint(one, pltpu.VMEM) for one in held))
    return uk, nk, fk.T, uv, nv, fv.T


def solution(mesh):
    wide = P("replica", "shard", None)
    flat = P("shard", None)
    return jax.shard_map(
        per_device,
        mesh=mesh,
        in_specs=(wide, wide, flat, wide, wide, flat),
        out_specs=(flat, wide, flat, flat, wide, flat),
        check_vma=False,
    )
```

```python
import functools

import jax
import jax.numpy as jnp
from jax import lax
from jax.experimental import pallas as pl
from jax.experimental.pallas import tpu as pltpu
from jax.sharding import PartitionSpec as P

MESH = pl.DeviceIdType.MESH
F32, BF16 = jnp.float32, jnp.bfloat16
NX, NY, NZ, NC = 4, 4, 8, 2
REPLICAS = 16
RANK = 64
ROWS = 64
BLK = 512
BLKS = 16
COL = 256
COLS = 32
RIDGE = 1e-6
LAG = 4
NT = (((1,), (1,)), ((), ()))
NN = (((1,), (0,)), ((), ()))


def device(x, y, z, c):
    return (lax.rem(y, 2) * NZ + z, (lax.div(y, 2) * NX + x) * NC + c)


def send(src, dst, ssem, rsem, dev):
    copy = pltpu.make_async_remote_copy(
        src_ref=src, dst_ref=dst, send_sem=ssem, recv_sem=rsem, device_id=dev, device_id_type=MESH
    )
    copy.start()
    return copy


def arrival(dst, ssem, rsem, dev):
    pltpu.make_async_remote_copy(
        src_ref=dst, dst_ref=dst, send_sem=ssem, recv_sem=rsem, device_id=dev, device_id_type=MESH
    ).wait_recv()


def solve_rows(gram, left):
    row = lax.broadcasted_iota(jnp.int32, (RANK, RANK), 0)
    lane = lax.broadcasted_iota(jnp.int32, (RANK, RANK), 1)
    diag = lane == row
    trace = jnp.sum(jnp.where(diag, gram, 0.0))
    rest = (gram + jnp.where(diag, RIDGE * (trace / RANK), 0.0), left)
    sub = lax.broadcasted_iota(jnp.int32, (8, 128), 0)
    done = ([], [])
    for t in range(8):
        count = RANK - 8 * t
        head = [one[:8] for one in rest]
        tail = [one[8:] if t < 7 else None for one in rest]
        cols = [jnp.broadcast_to(rest[0][:, 8 * t + k : 8 * t + k + 1], (count, 128)) for k in range(8)]
        hcol = [col[:8] for col in cols]
        tcol = [col[8:] if t < 7 else None for col in cols]
        for k in range(8):
            inv = 1.0 / hcol[k][k : k + 1, :]
            across = [hcol[j][k : k + 1, :] for j in range(8)]
            pivot = [one[k : k + 1, :] for one in head]
            if k < 7:
                m = jnp.where(sub > k, hcol[k] * inv, 0.0)
                for j in range(k + 1, 8):
                    hcol[j] = hcol[j] - m * across[j]
                head = [head[0] - m[:, :RANK] * pivot[0], head[1] - m * pivot[1]]
            if t < 7:
                m = tcol[k] * inv
                for j in range(k + 1, 8):
                    tcol[j] = tcol[j] - m * across[j]
                tail = [tail[0] - m[:, :RANK] * pivot[0], tail[1] - m * pivot[1]]
        for i in range(2):
            done[i].append(head[i])
        rest = tail
    pivots = jnp.sum(jnp.where(diag, jnp.concatenate(done[0], axis=0), 0.0), axis=1, keepdims=True)
    return jnp.concatenate(done[1], axis=0) * lax.rsqrt(pivots)


def step_kernel(
    gk, ek, pk, gv, ev, pv,
    uk, nk, fk, uv, nv, fv,
    grads, errors, mbuf, mchip, pstage, pbuf, acc, lbuf, r1, lt2, c1, obuf,
    wbuf, s1, r2, s2, r3, s3, r4, fbuf,
    load_sem, p_ss, p_rs, m_ss, m_rs, o_ss, o_rs,
    a_ss, a_rs, q_ss, q_rs, b_ss, b_rs, b2_ss, b2_rs, c1_ss, c1_rs,
    e1_ss, e1_rs, e2_ss, e2_rs, e3_ss, e3_rs,
    g3_ss, g3_rs, g2_ss, g2_rs, g1_ss, g1_rs, g0_ss, g0_rs,
):
    r = lax.axis_index("replica")
    s = lax.axis_index("shard")
    y_lo, z = lax.div(r, NZ), lax.rem(r, NZ)
    y_hi, x, c = lax.div(s, NX * NC), lax.rem(lax.div(s, NC), NX), lax.rem(s, NC)
    y = 2 * y_hi + y_lo
    oc = 1 - c
    cross = lax.rem(y + 3 + 2 * y_lo, NY)
    flip = 2 * y_hi + 1 - y_lo
    mate = device(x, y, z, oc)

    def at_x(d):
        return lax.rem(x + d, NX)

    def at_y(d):
        return lax.rem(y + d, NY)

    def at_z(d):
        return lax.rem(z + d, NZ)

    chip = y_hi * NX + x
    own_prev = [
        pltpu.make_async_copy(src.at[pl.ds(32 * h, 32)], pstage.at[m, h], load_sem.at[4 + 2 * m + h])
        for m, src in enumerate((pk, pv))
        for h in range(2)
    ]
    loads = [
        pltpu.make_async_copy(gk.at[0], grads.at[0], load_sem.at[0]),
        pltpu.make_async_copy(ek.at[0], errors.at[0], load_sem.at[1]),
        pltpu.make_async_copy(gv.at[0], grads.at[1], load_sem.at[2]),
        pltpu.make_async_copy(ev.at[0], errors.at[1], load_sem.at[3]),
    ]
    partners = [device(x, flip, at_z(d), c) for d in (4, 3, 5, 2, 6, 1, 7)]
    partners += [device(x, y, at_z(d), c) for d in (4, 3, 5, 2, 6, 1, 7)]
    partners += [device(at_x(d), cross, z, c) for d in (2, 1, 3)]
    partners += [device(at_x(d), y, z, c) for d in (2, 1, 3)]
    partners += [device(x, at_y(d), z, c) for d in (2, 1, 3)]
    partners += [mate]
    barrier = pltpu.get_barrier_semaphore()
    for dev in partners:
        pl.semaphore_signal(barrier, inc=1, device_id=dev, device_id_type=MESH)
    for copy in own_prev + loads:
        copy.start()
    for copy in own_prev:
        copy.wait()
    pl.semaphore_wait(barrier, len(partners))

    sent = []

    def take():
        old = sent[:]
        sent.clear()
        return old

    def settle(copies):
        for copy in copies:
            copy.wait_send()

    copy = send(pstage.at[oc], pbuf.at[chip, pl.ds(2 * c, 2)], p_ss, p_rs, mate)
    sent.append(copy)
    pbuf[chip, pl.ds(2 * c, 2)] = pstage[c]
    arrival(pbuf.at[chip, pl.ds(2 * oc, 2)], p_ss, p_rs, mate)
    far = [(2, 1), (1, 1), (3, 1), (2, 0), (1, 0), (3, 0), (0, 1)]

    def quarter(one, q):
        return pbuf.at[one, lax.rem(q, 4)]

    color = z + 2 * y_lo
    for i, (dx, over) in enumerate(far):
        dev = device(at_x(dx), cross if over else y, z, c)
        piece = quarter(chip, color + 2 * over)
        sent.append(send(piece, piece, a_ss.at[i], a_rs.at[i], dev))
    near = (device(x, flip, z, c), device(x, y, at_z(1), c), device(x, y, at_z(7), c))

    for copy in loads:
        copy.wait()

    def merge(b, carry):
        cols = pl.ds(pl.multiple_of(b * COL, COL), COL)
        for m in range(2):
            total = grads[m, :, cols].astype(F32) + errors[m, :, cols].astype(F32)
            mbuf[m, b] = total.astype(BF16)
        mchip[c, b] = mbuf[c, b]
        return carry

    lax.fori_loop(0, COLS, merge, 0)
    for t in range(4):
        part = pl.ds(8 * t, 8)
        sent.append(send(mbuf.at[oc, part], mchip.at[c, part], m_ss.at[t], m_rs.at[t], mate))

    def block_of(b):
        return jnp.concatenate([mchip[0, b], mchip[1, b]], axis=0)

    def left_term(one):
        total = None
        for bit in range(2):
            for h in range(2):
                cols = slice(h * COL, h * COL + COL)
                prev = jnp.concatenate([pbuf[one, 2 * bit, :, cols], pbuf[one, 2 * bit + 1, :, cols]], axis=0)
                term = lax.dot_general(prev, block_of(4 * one + 2 * bit + h), NT, preferred_element_type=F32)
                total = term if total is None else total + term
        return total

    order = (4, 5, 6, 1, 2, 3, 0)
    chips = []
    for i, (dx, over) in enumerate(far):
        yy = (1 - y_hi) if over else y_hi
        chips.append(yy * NX + lax.rem(x + NX - dx, NX))
    for i in order:
        piece = quarter(chips[i], color)
        arrival(piece, a_ss.at[i], a_rs.at[i], mate)
        for n in range(3):
            sent.append(send(piece, piece, q_ss.at[i, n], q_rs.at[i, n], near[n]))
    for t in range(4):
        arrival(mchip.at[oc, pl.ds(8 * t, 8)], m_ss.at[t], m_rs.at[t], mate)
    acc[...] = left_term(chip)
    for i in order:
        for n in range(3):
            arrival(quarter(chips[i], color + (2, 3, 1)[n]), q_ss.at[i, n], q_rs.at[i, n], mate)
        acc[...] += left_term(chips[i])

    for t in range(NZ):
        lbuf[t] = acc[8 * t : 8 * t + 8, :]
    r1[r] = lbuf[z]
    old = take()
    peers = [(1, d) for d in (4, 3, 5, 2, 6, 1, 7, 0)] + [(0, d) for d in (4, 3, 5, 2, 6, 1, 7)]
    for i, (over, dz) in enumerate(peers):
        dev = device(x, flip if over else y, at_z(dz), c)
        sent.append(send(lbuf.at[at_z(dz)], r1.at[r], b_ss.at[i], b_rs.at[i], dev))
    settle(old)
    for i, (over, dz) in enumerate(peers):
        slot = ((1 - y_lo) if over else y_lo) * NZ + lax.rem(z + NZ - dz, NZ)
        arrival(r1.at[slot], b_ss.at[i], b_rs.at[i], mate)
    total = r1[0]
    for t in range(1, REPLICAS):
        total = total + r1[t]
    lt2[z] = total / REPLICAS
    zs = (4, 3, 5, 2, 6, 1, 7)
    old = take()
    for i, dz in enumerate(zs):
        sent.append(send(lt2.at[z], lt2.at[z], b2_ss.at[i], b2_rs.at[i], device(x, y, at_z(dz), c)))
    settle(old)
    for i, dz in enumerate(zs):
        arrival(lt2.at[lax.rem(z + NZ - dz, NZ)], b2_ss.at[i], b2_rs.at[i], mate)

    left = jnp.concatenate([lt2[t] for t in range(NZ)], axis=0)
    gram = lax.dot_general(left, left, NT, precision=lax.Precision.HIGHEST, preferred_element_type=F32)
    c1[chip] = jnp.concatenate([gram[0:32], gram[32:64]], axis=1)
    old = take()
    for i, (dx, over) in enumerate(far):
        dev = device(at_x(dx), cross if over else y, z, c)
        sent.append(send(c1.at[chip], c1.at[chip], c1_ss.at[i], c1_rs.at[i], dev))
    settle(old)
    for i in range(7):
        arrival(c1.at[chips[i]], c1_ss.at[i], c1_rs.at[i], mate)
    total = c1[0]
    for t in range(1, 8):
        total = total + c1[t]
    gram = jnp.concatenate([total[:, :RANK], total[:, RANK:]], axis=0)

    ortho = solve_rows(gram, left).astype(BF16)
    obuf[c] = ortho
    old = take()
    copy = send(obuf.at[c], obuf.at[c], o_ss, o_rs, mate)
    sent.append(copy)

    firsts = (x, y)
    seconds = (y, x)
    ds = (2, 1, 3, 0)

    def first(pq, d):
        return lax.rem(firsts[pq] + d, 4)

    def second(pq, d):
        return lax.rem(seconds[pq] + d, 4)

    def dev1(pq, d):
        return device(at_x(d), y, z, c) if pq == 0 else device(x, at_y(d), z, c)

    def dev2(pq, d):
        return device(x, at_y(d), z, c) if pq == 0 else device(at_x(d), y, z, c)

    for j, dj in enumerate(ds):
        for pq in range(2):
            i2 = second(pq, dj)
            for k, dk in enumerate(ds):
                block = block_of(pq * 16 + first(pq, dk) * 4 + i2)
                term = lax.dot_general(ortho, block, NN, preferred_element_type=F32)
                for a in range(4):
                    for b in range(2):
                        tile = term[16 * a : 16 * a + 16, b * 128 : b * 128 + 128]
                        if dk == 0:
                            wbuf[pq, j, 2 * a + b] = tile
                        else:
                            s1[pq, j, k, 2 * a + b] = tile.astype(BF16)
                if dk != 0:
                    sent.append(
                        send(s1.at[pq, j, k], r2.at[pq, j, k], e1_ss.at[pq, j, k], e1_rs.at[pq, j, k], dev1(pq, dk))
                    )
    settle(old)
    for j, dj in enumerate(ds):
        for pq in range(2):
            total = wbuf[pq, j]
            for k in range(3):
                arrival(r2.at[pq, j, k], e1_ss.at[pq, j, k], e1_rs.at[pq, j, k], mate)
                total = total + r2[pq, j, k].astype(F32)
            if dj == 0:
                wbuf[pq, j] = total
            else:
                s2[pq, j] = total.astype(BF16)
                sent.append(
                    send(s2.at[pq, j], r3.at[pq, j], e2_ss.at[pq, j], e2_rs.at[pq, j], dev2(pq, dj))
                )
    settle(take())
    for pq in range(2):
        total = wbuf[pq, 3]
        for j in range(3):
            arrival(r3.at[pq, j], e2_ss.at[pq, j], e2_rs.at[pq, j], mate)
            total = total + r3[pq, j].astype(F32)
        wbuf[pq, 3] = total
        s3[:, pq] = total.astype(BF16)
    old = take()
    for i, dz in enumerate(zs):
        there = at_z(dz)
        sent.append(send(s3.at[there], r4.at[i], e3_ss.at[i], e3_rs.at[i], device(x, y, there, c)))
    settle(old)
    last = take()
    for i in range(7):
        arrival(r4.at[i], e3_ss.at[i], e3_rs.at[i], mate)
    for pq in range(2):
        i1, i2 = first(pq, 0), second(pq, 0)
        total = wbuf[pq, 3, z]
        for i in range(7):
            total = total + r4[i, pq].astype(F32)
        fbuf[c, pq, i1, i2, z] = (total / REPLICAS).astype(BF16)

    for pq in range(2):
        piece = fbuf.at[c, pq, first(pq, 0), second(pq, 0), z]
        for i, dz in enumerate(zs):
            sent.append(send(piece, piece, g3_ss.at[pq, i], g3_rs.at[pq, i], device(x, y, at_z(dz), c)))
    settle(last)
    last = take()
    arrival(obuf.at[oc], o_ss, o_rs, mate)
    wide = []
    for m in range(2):
        turned = obuf[m].astype(F32).T
        turned = jnp.where(c == 0, turned[:ROWS], turned[ROWS:])
        none = jnp.zeros((ROWS, RANK), F32)
        wide.append(jnp.concatenate([turned, none] if m == 0 else [none, turned], axis=1))
    wide = jnp.concatenate(wide, axis=0).astype(BF16)

    def sub_piece(pq, k, j):
        return fbuf.at[c, pq, first(pq, 4 - ds[k]), second(pq, 4 - ds[j])]

    def pass_on(pq, k, j):
        piece = sub_piece(pq, k, j)
        sent.append(send(piece, piece, g0_ss.at[pq, k, j], g0_rs.at[pq, k, j], mate))
        chunks.append((pq, k, j))

    def spread(pq, j):
        piece = sub_piece(pq, 3, j)
        for k in range(3):
            sent.append(send(piece, piece, g1_ss.at[pq, j, k], g1_rs.at[pq, j, k], dev1(pq, ds[k])))
        pass_on(pq, 3, j)

    def finish(pq, k, j):
        i1, i2 = first(pq, 4 - ds[k]), second(pq, 4 - ds[j])
        arrival(fbuf.at[oc, pq, i1, i2], g0_ss.at[pq, k, j], g0_rs.at[pq, k, j], mate)
        sides = []
        for m in range(2):
            tiles = fbuf[m, pq, i1, i2]
            rows = [jnp.concatenate([tiles[2 * a], tiles[2 * a + 1]], axis=1) for a in range(4)]
            sides.append(jnp.concatenate(rows, axis=0))
        factor = jnp.concatenate(sides, axis=0)
        approx = lax.dot_general(wide, factor, NN, preferred_element_type=F32)
        block = pq * 16 + i1 * 4 + i2
        merged = jnp.concatenate([mbuf[0, block], mbuf[1, block]], axis=0)
        rest = (merged.astype(F32) - approx).astype(BF16)
        approx = approx.astype(BF16)
        cols = pl.ds(pl.multiple_of(block * COL, COL), COL)
        for m, (u, e) in enumerate(((uk, nk), (uv, nv))):
            u[:, cols] = approx[m * ROWS : m * ROWS + ROWS]
            e[0, :, cols] = rest[m * ROWS : m * ROWS + ROWS]

    chunks = []
    for pq in range(2):
        piece = sub_piece(pq, 3, 3)
        for i, dz in enumerate(zs):
            arrival(
                fbuf.at[c, pq, first(pq, 0), second(pq, 0), lax.rem(z + NZ - dz, NZ)],
                g3_ss.at[pq, i], g3_rs.at[pq, i], mate,
            )
        for k in range(3):
            sent.append(send(piece, piece, g2_ss.at[pq, k], g2_rs.at[pq, k], dev2(pq, ds[k])))
        spread(pq, 3)
    settle(last)
    for j in (1, 2, 0):
        for pq in range(2):
            arrival(sub_piece(pq, 3, j), g2_ss.at[pq, j], g2_rs.at[pq, j], mate)
            spread(pq, j)
    for j in (3, 1, 2, 0):
        for pq in range(2):
            for k in (1, 2, 0):
                arrival(sub_piece(pq, k, j), g1_ss.at[pq, j, k], g1_rs.at[pq, j, k], mate)
                pass_on(pq, k, j)
                if len(chunks) > LAG:
                    finish(*chunks.pop(0))
    while chunks:
        finish(*chunks.pop(0))
    for i in range(2):
        for m in range(2):
            rows = [
                jnp.concatenate([fbuf[m, s // 8, s % 8 // 2, s % 2 * 2 + i, 2 * a + b] for b in range(2)], axis=1)
                for a in range(4)
            ]
            (fk, fv)[m][:, i * COL : (i + 1) * COL] = jnp.concatenate(rows, axis=0).astype(F32)
    for copy in sent:
        copy.wait_send()


def flush_kernel(uk, nk, fk, uv, nv, fv, uk_out, nk_out, fk_out, uv_out, nv_out, fv_out, sems):
    pairs = [(fk, fk_out), (fv, fv_out)]
    for q in range(4):
        rows = pl.ds(16 * q, 16)
        pairs += [(uk.at[rows], uk_out.at[rows]), (uv.at[rows], uv_out.at[rows])]
        pairs += [(nk.at[0, rows], nk_out.at[0, rows]), (nv.at[0, rows], nv_out.at[0, rows])]
    copies = [pltpu.make_async_copy(src, dst, sems.at[i]) for i, (src, dst) in enumerate(pairs)]
    for copy in copies:
        copy.start()
    for copy in copies:
        copy.wait()


def per_device(grad_key, error_key, prev_key, grad_val, error_val, prev_val):
    vm = pltpu.VMEM
    dma = pltpu.SemaphoreType.DMA
    scratch = [
        vm((2, ROWS, 8192), BF16), vm((2, ROWS, 8192), BF16),
        vm((2, COLS, ROWS, COL), BF16), vm((2, COLS, ROWS, COL), BF16),
        vm((2, 2, 32, BLK), BF16), vm((8, 4, 32, BLK), BF16),
        vm((RANK, 128), F32), vm((8, 8, 128), F32), vm((16, 8, 128), F32), vm((8, 8, 128), F32),
        vm((8, 32, 128), F32), vm((2, RANK, 128), BF16),
        vm((2, 4, 8, 16, 128), F32),
        vm((2, 4, 3, 8, 16, 128), BF16), vm((2, 4, 3, 8, 16, 128), BF16),
        vm((2, 3, 8, 16, 128), BF16), vm((2, 3, 8, 16, 128), BF16),
        vm((8, 2, 16, 128), BF16), vm((7, 2, 16, 128), BF16),
        vm((2, 2, 4, 4, 8, 16, 128), BF16),
        dma((8,)),
    ]
    for n in (
        None, (4,), None, (7,), (7, 3), (15,), (7,), (7,),
        (2, 4, 3), (2, 3), (7,), (2, 7), (2, 3), (2, 4, 3), (2, 4, 4),
    ):
        for _ in range(2):
            scratch.append(dma if n is None else dma(n))
    hbm = pl.BlockSpec(memory_space=pl.ANY)
    out = pl.BlockSpec(memory_space=pltpu.VMEM)
    shapes = [((ROWS, 8192), BF16), ((1, ROWS, 8192), BF16), ((RANK, BLK), F32)] * 2
    operands = (grad_key, error_key, prev_key.T, grad_val, error_val, prev_val.T)
    held = pl.pallas_call(
        step_kernel,
        name="exchange",
        out_shape=tuple(pltpu.VMEM(*one) for one in shapes),
        in_specs=[hbm] * 6,
        out_specs=(out,) * 6,
        scratch_shapes=scratch,
        compiler_params=pltpu.CompilerParams(
            collective_id=0, has_side_effects=True, vmem_limit_bytes=32 * 2**20
        ),
    )(*(pltpu.with_memory_space_constraint(one, pltpu.HBM) for one in operands))
    uk, nk, fk, uv, nv, fv = pl.pallas_call(
        flush_kernel,
        name="flush",
        out_shape=tuple(jax.ShapeDtypeStruct(*one) for one in shapes),
        in_specs=[pl.BlockSpec(memory_space=pltpu.VMEM)] * 6,
        out_specs=(hbm,) * 6,
        scratch_shapes=[dma((20,))],
        compiler_params=pltpu.CompilerParams(vmem_limit_bytes=2**21),
    )(*(pltpu.with_memory_space_constraint(one, pltpu.VMEM) for one in held))
    return uk, nk, fk.T, uv, nv, fv.T


def solution(mesh):
    wide = P("replica", "shard", None)
    flat = P("shard", None)
    return jax.shard_map(
        per_device,
        mesh=mesh,
        in_specs=(wide, wide, flat, wide, wide, flat),
        out_specs=(flat, wide, flat, flat, wide, flat),
        check_vma=False,
    )
```

```python
import functools

import jax
import jax.numpy as jnp
from jax import lax
from jax.experimental import pallas as pl
from jax.experimental.pallas import tpu as pltpu
from jax.sharding import PartitionSpec as P

MESH = pl.DeviceIdType.MESH
F32, BF16 = jnp.float32, jnp.bfloat16
NX, NY, NZ, NC = 4, 4, 8, 2
REPLICAS = 16
RANK = 64
ROWS = 64
BLK = 512
BLKS = 16
COL = 256
COLS = 32
RIDGE = 1e-6
LAG = 4
NT = (((1,), (1,)), ((), ()))
NN = (((1,), (0,)), ((), ()))


def device(x, y, z, c):
    return (lax.rem(y, 2) * NZ + z, (lax.div(y, 2) * NX + x) * NC + c)


def send(src, dst, ssem, rsem, dev):
    copy = pltpu.make_async_remote_copy(
        src_ref=src, dst_ref=dst, send_sem=ssem, recv_sem=rsem, device_id=dev, device_id_type=MESH
    )
    copy.start()
    return copy


def arrival(dst, ssem, rsem, dev):
    pltpu.make_async_remote_copy(
        src_ref=dst, dst_ref=dst, send_sem=ssem, recv_sem=rsem, device_id=dev, device_id_type=MESH
    ).wait_recv()


def solve_rows(gram, left):
    row = lax.broadcasted_iota(jnp.int32, (RANK, RANK), 0)
    lane = lax.broadcasted_iota(jnp.int32, (RANK, RANK), 1)
    diag = lane == row
    trace = jnp.sum(jnp.where(diag, gram, 0.0))
    rest = (gram + jnp.where(diag, RIDGE * (trace / RANK), 0.0), left)
    sub = lax.broadcasted_iota(jnp.int32, (8, 128), 0)
    done = ([], [])
    for t in range(8):
        count = RANK - 8 * t
        head = [one[:8] for one in rest]
        tail = [one[8:] if t < 7 else None for one in rest]
        cols = [jnp.broadcast_to(rest[0][:, 8 * t + k : 8 * t + k + 1], (count, 128)) for k in range(8)]
        hcol = [col[:8] for col in cols]
        tcol = [col[8:] if t < 7 else None for col in cols]
        for k in range(8):
            inv = 1.0 / hcol[k][k : k + 1, :]
            across = [hcol[j][k : k + 1, :] for j in range(8)]
            pivot = [one[k : k + 1, :] for one in head]
            if k < 7:
                m = jnp.where(sub > k, hcol[k] * inv, 0.0)
                for j in range(k + 1, 8):
                    hcol[j] = hcol[j] - m * across[j]
                head = [head[0] - m[:, :RANK] * pivot[0], head[1] - m * pivot[1]]
            if t < 7:
                m = tcol[k] * inv
                for j in range(k + 1, 8):
                    tcol[j] = tcol[j] - m * across[j]
                tail = [tail[0] - m[:, :RANK] * pivot[0], tail[1] - m * pivot[1]]
        for i in range(2):
            done[i].append(head[i])
        rest = tail
    pivots = jnp.sum(jnp.where(diag, jnp.concatenate(done[0], axis=0), 0.0), axis=1, keepdims=True)
    return jnp.concatenate(done[1], axis=0) * lax.rsqrt(pivots)


def step_kernel(
    gk, ek, pk, gv, ev, pv,
    uk, nk, fk, uv, nv, fv,
    grads, errors, mbuf, mchip, pstage, pbuf, acc, lbuf, r1, lt2, c1, obuf,
    wbuf, s1, r2, s2, r3, s3, r4, fbuf,
    load_sem, p_ss, p_rs, m_ss, m_rs, o_ss, o_rs,
    a_ss, a_rs, q_ss, q_rs, b_ss, b_rs, b2_ss, b2_rs, c1_ss, c1_rs,
    e1_ss, e1_rs, e2_ss, e2_rs, e3_ss, e3_rs,
    g3_ss, g3_rs, g2_ss, g2_rs, g1_ss, g1_rs, g0_ss, g0_rs,
):
    r = lax.axis_index("replica")
    s = lax.axis_index("shard")
    y_lo, z = lax.div(r, NZ), lax.rem(r, NZ)
    y_hi, x, c = lax.div(s, NX * NC), lax.rem(lax.div(s, NC), NX), lax.rem(s, NC)
    y = 2 * y_hi + y_lo
    oc = 1 - c
    cross = lax.rem(y + 3 + 2 * y_lo, NY)
    flip = 2 * y_hi + 1 - y_lo
    mate = device(x, y, z, oc)

    def at_x(d):
        return lax.rem(x + d, NX)

    def at_y(d):
        return lax.rem(y + d, NY)

    def at_z(d):
        return lax.rem(z + d, NZ)

    chip = y_hi * NX + x
    own_prev = [
        pltpu.make_async_copy(src.at[pl.ds(32 * h, 32)], pstage.at[m, h], load_sem.at[4 + 2 * m + h])
        for m, src in enumerate((pk, pv))
        for h in range(2)
    ]
    loads = [
        pltpu.make_async_copy(gk.at[0], grads.at[0], load_sem.at[0]),
        pltpu.make_async_copy(ek.at[0], errors.at[0], load_sem.at[1]),
        pltpu.make_async_copy(gv.at[0], grads.at[1], load_sem.at[2]),
        pltpu.make_async_copy(ev.at[0], errors.at[1], load_sem.at[3]),
    ]
    partners = [device(x, flip, at_z(d), c) for d in (4, 3, 5, 2, 6, 1, 7)]
    partners += [device(x, y, at_z(d), c) for d in (4, 3, 5, 2, 6, 1, 7)]
    partners += [device(at_x(d), cross, z, c) for d in (2, 1, 3)]
    partners += [device(at_x(d), y, z, c) for d in (2, 1, 3)]
    partners += [device(x, at_y(d), z, c) for d in (2, 1, 3)]
    partners += [device(at_x(d), cross, z, oc) for d in (2, 1, 3, 0)]
    partners += [device(at_x(d), y, z, oc) for d in (2, 1, 3)]
    partners += [mate]
    barrier = pltpu.get_barrier_semaphore()
    for dev in partners:
        pl.semaphore_signal(barrier, inc=1, device_id=dev, device_id_type=MESH)
    for copy in own_prev + loads:
        copy.start()
    for copy in own_prev:
        copy.wait()
    pl.semaphore_wait(barrier, len(partners))

    sent = []

    def take():
        old = sent[:]
        sent.clear()
        return old

    def settle(copies):
        for copy in copies:
            copy.wait_send()

    far = [(2, 1), (1, 1), (3, 1), (2, 0), (1, 0), (3, 0), (0, 1)]

    def quarter(one, q):
        return pbuf.at[one, lax.rem(q, 4)]

    color = z + 2 * y_lo
    along = c == lax.rem(lax.div(color, 2), 2)
    half = lax.rem(color, 2)
    row = jnp.where(along, y, cross)
    there = quarter(chip, color + jnp.where(along, 0, 2))
    place = jnp.where(along, 3, 0)
    for i in range(3):
        for m in range(2):
            dev = device(at_x(far[i][0]), row, z, m)
            sent.append(send(pstage.at[m, half], there, a_ss.at[m, i], a_rs.at[place + i], dev))

    @pl.when(jnp.logical_not(along))
    def _():
        for m in range(2):
            send(pstage.at[m, half], there, a_ss.at[m, 3], a_rs.at[6], device(x, cross, z, m))

    copy = send(pstage.at[oc], pbuf.at[chip, pl.ds(2 * c, 2)], p_ss, p_rs, mate)
    sent.append(copy)
    pbuf[chip, pl.ds(2 * c, 2)] = pstage[c]
    near = (device(x, flip, z, c), device(x, y, at_z(1), c), device(x, y, at_z(7), c))

    for copy in loads:
        copy.wait()

    def merge(b, carry):
        cols = pl.ds(pl.multiple_of(b * COL, COL), COL)
        for m in range(2):
            total = grads[m, :, cols].astype(F32) + errors[m, :, cols].astype(F32)
            mbuf[m, b] = total.astype(BF16)
        mchip[c, b] = mbuf[c, b]
        return carry

    lax.fori_loop(0, COLS, merge, 0)
    for t in range(4):
        part = pl.ds(8 * t, 8)
        sent.append(send(mbuf.at[oc, part], mchip.at[c, part], m_ss.at[t], m_rs.at[t], mate))

    def block_of(b):
        return jnp.concatenate([mchip[0, b], mchip[1, b]], axis=0)

    def left_term(one):
        total = None
        for bit in range(2):
            for h in range(2):
                cols = slice(h * COL, h * COL + COL)
                prev = jnp.concatenate([pbuf[one, 2 * bit, :, cols], pbuf[one, 2 * bit + 1, :, cols]], axis=0)
                term = lax.dot_general(prev, block_of(4 * one + 2 * bit + h), NT, preferred_element_type=F32)
                total = term if total is None else total + term
        return total

    order = (4, 5, 6, 1, 2, 3, 0)
    chips = []
    for i, (dx, over) in enumerate(far):
        yy = (1 - y_hi) if over else y_hi
        chips.append(yy * NX + lax.rem(x + NX - dx, NX))
    for i in order:
        piece = quarter(chips[i], color)
        arrival(piece, a_ss.at[i], a_rs.at[i], mate)
        for n in range(3):
            sent.append(send(piece, piece, q_ss.at[i, n], q_rs.at[i, n], near[n]))
    for t in range(4):
        arrival(mchip.at[oc, pl.ds(8 * t, 8)], m_ss.at[t], m_rs.at[t], mate)
    arrival(pbuf.at[chip, pl.ds(2 * oc, 2)], p_ss, p_rs, mate)
    acc[...] = left_term(chip)
    for i in order:
        for n in range(3):
            arrival(quarter(chips[i], color + (2, 3, 1)[n]), q_ss.at[i, n], q_rs.at[i, n], mate)
        acc[...] += left_term(chips[i])

    @pl.when(jnp.logical_not(along))
    def _():
        for m in range(2):
            pltpu.make_async_remote_copy(
                src_ref=pstage.at[m, half], dst_ref=there, send_sem=a_ss.at[m, 3], recv_sem=a_rs.at[6],
                device_id=mate, device_id_type=MESH,
            ).wait_send()

    for t in range(NZ):
        lbuf[t] = acc[8 * t : 8 * t + 8, :]
    r1[r] = lbuf[z]
    old = take()
    peers = [(1, d) for d in (4, 3, 5, 2, 6, 1, 7, 0)] + [(0, d) for d in (4, 3, 5, 2, 6, 1, 7)]
    for i, (over, dz) in enumerate(peers):
        dev = device(x, flip if over else y, at_z(dz), c)
        sent.append(send(lbuf.at[at_z(dz)], r1.at[r], b_ss.at[i], b_rs.at[i], dev))
    settle(old)
    for i, (over, dz) in enumerate(peers):
        slot = ((1 - y_lo) if over else y_lo) * NZ + lax.rem(z + NZ - dz, NZ)
        arrival(r1.at[slot], b_ss.at[i], b_rs.at[i], mate)
    total = r1[0]
    for t in range(1, REPLICAS):
        total = total + r1[t]
    lt2[z] = total / REPLICAS
    zs = (4, 3, 5, 2, 6, 1, 7)
    old = take()
    for i, dz in enumerate(zs):
        sent.append(send(lt2.at[z], lt2.at[z], b2_ss.at[i], b2_rs.at[i], device(x, y, at_z(dz), c)))
    settle(old)
    for i, dz in enumerate(zs):
        arrival(lt2.at[lax.rem(z + NZ - dz, NZ)], b2_ss.at[i], b2_rs.at[i], mate)

    left = jnp.concatenate([lt2[t] for t in range(NZ)], axis=0)
    gram = lax.dot_general(left, left, NT, precision=lax.Precision.HIGHEST, preferred_element_type=F32)
    c1[chip] = jnp.concatenate([gram[0:32], gram[32:64]], axis=1)
    old = take()
    for i, (dx, over) in enumerate(far):
        dev = device(at_x(dx), cross if over else y, z, c)
        sent.append(send(c1.at[chip], c1.at[chip], c1_ss.at[i], c1_rs.at[i], dev))
    settle(old)
    for i in range(7):
        arrival(c1.at[chips[i]], c1_ss.at[i], c1_rs.at[i], mate)
    total = c1[0]
    for t in range(1, 8):
        total = total + c1[t]
    gram = jnp.concatenate([total[:, :RANK], total[:, RANK:]], axis=0)

    ortho = solve_rows(gram, left).astype(BF16)
    obuf[c] = ortho
    old = take()
    copy = send(obuf.at[c], obuf.at[c], o_ss, o_rs, mate)
    sent.append(copy)

    firsts = (x, y)
    seconds = (y, x)
    ds = (2, 1, 3, 0)

    def first(pq, d):
        return lax.rem(firsts[pq] + d, 4)

    def second(pq, d):
        return lax.rem(seconds[pq] + d, 4)

    def dev1(pq, d):
        return device(at_x(d), y, z, c) if pq == 0 else device(x, at_y(d), z, c)

    def dev2(pq, d):
        return device(x, at_y(d), z, c) if pq == 0 else device(at_x(d), y, z, c)

    for j, dj in enumerate(ds):
        for pq in range(2):
            i2 = second(pq, dj)
            for k, dk in enumerate(ds):
                block = block_of(pq * 16 + first(pq, dk) * 4 + i2)
                term = lax.dot_general(ortho, block, NN, preferred_element_type=F32)
                for a in range(4):
                    for b in range(2):
                        tile = term[16 * a : 16 * a + 16, b * 128 : b * 128 + 128]
                        if dk == 0:
                            wbuf[pq, j, 2 * a + b] = tile
                        else:
                            s1[pq, j, k, 2 * a + b] = tile.astype(BF16)
                if dk != 0:
                    sent.append(
                        send(s1.at[pq, j, k], r2.at[pq, j, k], e1_ss.at[pq, j, k], e1_rs.at[pq, j, k], dev1(pq, dk))
                    )
    settle(old)
    for j, dj in enumerate(ds):
        for pq in range(2):
            total = wbuf[pq, j]
            for k in range(3):
                arrival(r2.at[pq, j, k], e1_ss.at[pq, j, k], e1_rs.at[pq, j, k], mate)
                total = total + r2[pq, j, k].astype(F32)
            if dj == 0:
                wbuf[pq, j] = total
            else:
                s2[pq, j] = total.astype(BF16)
                sent.append(
                    send(s2.at[pq, j], r3.at[pq, j], e2_ss.at[pq, j], e2_rs.at[pq, j], dev2(pq, dj))
                )
    settle(take())
    for pq in range(2):
        total = wbuf[pq, 3]
        for j in range(3):
            arrival(r3.at[pq, j], e2_ss.at[pq, j], e2_rs.at[pq, j], mate)
            total = total + r3[pq, j].astype(F32)
        wbuf[pq, 3] = total
        s3[:, pq] = total.astype(BF16)
    old = take()
    for i, dz in enumerate(zs):
        there = at_z(dz)
        sent.append(send(s3.at[there], r4.at[i], e3_ss.at[i], e3_rs.at[i], device(x, y, there, c)))
    settle(old)
    last = take()
    for i in range(7):
        arrival(r4.at[i], e3_ss.at[i], e3_rs.at[i], mate)
    for pq in range(2):
        i1, i2 = first(pq, 0), second(pq, 0)
        total = wbuf[pq, 3, z]
        for i in range(7):
            total = total + r4[i, pq].astype(F32)
        fbuf[c, pq, i1, i2, z] = (total / REPLICAS).astype(BF16)

    for pq in range(2):
        piece = fbuf.at[c, pq, first(pq, 0), second(pq, 0), z]
        for i, dz in enumerate(zs):
            sent.append(send(piece, piece, g3_ss.at[pq, i], g3_rs.at[pq, i], device(x, y, at_z(dz), c)))
    settle(last)
    last = take()
    arrival(obuf.at[oc], o_ss, o_rs, mate)
    wide = []
    for m in range(2):
        turned = obuf[m].astype(F32).T
        turned = jnp.where(c == 0, turned[:ROWS], turned[ROWS:])
        none = jnp.zeros((ROWS, RANK), F32)
        wide.append(jnp.concatenate([turned, none] if m == 0 else [none, turned], axis=1))
    wide = jnp.concatenate(wide, axis=0).astype(BF16)

    def sub_piece(pq, k, j):
        return fbuf.at[c, pq, first(pq, 4 - ds[k]), second(pq, 4 - ds[j])]

    def pass_on(pq, k, j):
        piece = sub_piece(pq, k, j)
        sent.append(send(piece, piece, g0_ss.at[pq, k, j], g0_rs.at[pq, k, j], mate))
        chunks.append((pq, k, j))

    def spread(pq, j):
        piece = sub_piece(pq, 3, j)
        for k in range(3):
            sent.append(send(piece, piece, g1_ss.at[pq, j, k], g1_rs.at[pq, j, k], dev1(pq, ds[k])))
        pass_on(pq, 3, j)

    def finish(pq, k, j):
        i1, i2 = first(pq, 4 - ds[k]), second(pq, 4 - ds[j])
        arrival(fbuf.at[oc, pq, i1, i2], g0_ss.at[pq, k, j], g0_rs.at[pq, k, j], mate)
        sides = []
        for m in range(2):
            tiles = fbuf[m, pq, i1, i2]
            rows = [jnp.concatenate([tiles[2 * a], tiles[2 * a + 1]], axis=1) for a in range(4)]
            sides.append(jnp.concatenate(rows, axis=0))
        factor = jnp.concatenate(sides, axis=0)
        approx = lax.dot_general(wide, factor, NN, preferred_element_type=F32)
        block = pq * 16 + i1 * 4 + i2
        merged = jnp.concatenate([mbuf[0, block], mbuf[1, block]], axis=0)
        rest = (merged.astype(F32) - approx).astype(BF16)
        approx = approx.astype(BF16)
        cols = pl.ds(pl.multiple_of(block * COL, COL), COL)
        for m, (u, e) in enumerate(((uk, nk), (uv, nv))):
            u[:, cols] = approx[m * ROWS : m * ROWS + ROWS]
            e[0, :, cols] = rest[m * ROWS : m * ROWS + ROWS]

    def settle_some():
        for _ in range(min(3, len(sent) - 6)):
            sent.pop(0).wait_send()

    chunks = []
    for pq in range(2):
        piece = sub_piece(pq, 3, 3)
        for i, dz in enumerate(zs):
            arrival(
                fbuf.at[c, pq, first(pq, 0), second(pq, 0), lax.rem(z + NZ - dz, NZ)],
                g3_ss.at[pq, i], g3_rs.at[pq, i], mate,
            )
        for k in range(3):
            sent.append(send(piece, piece, g2_ss.at[pq, k], g2_rs.at[pq, k], dev2(pq, ds[k])))
        spread(pq, 3)
    settle(last)
    for j in (1, 2, 0):
        for pq in range(2):
            arrival(sub_piece(pq, 3, j), g2_ss.at[pq, j], g2_rs.at[pq, j], mate)
            spread(pq, j)
    for j in (3, 1, 2, 0):
        for pq in range(2):
            for k in (1, 2, 0):
                arrival(sub_piece(pq, k, j), g1_ss.at[pq, j, k], g1_rs.at[pq, j, k], mate)
                pass_on(pq, k, j)
                settle_some()
                if len(chunks) > LAG:
                    finish(*chunks.pop(0))
    while chunks:
        settle_some()
        finish(*chunks.pop(0))
    for i in range(2):
        for m in range(2):
            rows = [
                jnp.concatenate([fbuf[m, s // 8, s % 8 // 2, s % 2 * 2 + i, 2 * a + b] for b in range(2)], axis=1)
                for a in range(4)
            ]
            (fk, fv)[m][:, i * COL : (i + 1) * COL] = jnp.concatenate(rows, axis=0).astype(F32)
    for copy in sent:
        copy.wait_send()


def flush_kernel(uk, nk, fk, uv, nv, fv, uk_out, nk_out, fk_out, uv_out, nv_out, fv_out, sems):
    pairs = [(fk, fk_out), (fv, fv_out)]
    for q in range(4):
        rows = pl.ds(16 * q, 16)
        pairs += [(uk.at[rows], uk_out.at[rows]), (uv.at[rows], uv_out.at[rows])]
        pairs += [(nk.at[0, rows], nk_out.at[0, rows]), (nv.at[0, rows], nv_out.at[0, rows])]
    copies = [pltpu.make_async_copy(src, dst, sems.at[i]) for i, (src, dst) in enumerate(pairs)]
    for copy in copies:
        copy.start()
    for copy in copies:
        copy.wait()


def per_device(grad_key, error_key, prev_key, grad_val, error_val, prev_val):
    vm = pltpu.VMEM
    dma = pltpu.SemaphoreType.DMA
    scratch = [
        vm((2, ROWS, 8192), BF16), vm((2, ROWS, 8192), BF16),
        vm((2, COLS, ROWS, COL), BF16), vm((2, COLS, ROWS, COL), BF16),
        vm((2, 2, 32, BLK), BF16), vm((8, 4, 32, BLK), BF16),
        vm((RANK, 128), F32), vm((8, 8, 128), F32), vm((16, 8, 128), F32), vm((8, 8, 128), F32),
        vm((8, 32, 128), F32), vm((2, RANK, 128), BF16),
        vm((2, 4, 8, 16, 128), F32),
        vm((2, 4, 3, 8, 16, 128), BF16), vm((2, 4, 3, 8, 16, 128), BF16),
        vm((2, 3, 8, 16, 128), BF16), vm((2, 3, 8, 16, 128), BF16),
        vm((8, 2, 16, 128), BF16), vm((7, 2, 16, 128), BF16),
        vm((2, 2, 4, 4, 8, 16, 128), BF16),
        dma((8,)),
    ]
    for n in (
        None, None, (4,), (4,), None, None, (2, 4), (7,), (7, 3), (7, 3), (15,), (15,), (7,), (7,), (7,), (7,),
        (2, 4, 3), (2, 4, 3), (2, 3), (2, 3), (7,), (7,),
        (2, 7), (2, 7), (2, 3), (2, 3), (2, 4, 3), (2, 4, 3), (2, 4, 4), (2, 4, 4),
    ):
        scratch.append(dma if n is None else dma(n))
    hbm = pl.BlockSpec(memory_space=pl.ANY)
    out = pl.BlockSpec(memory_space=pltpu.VMEM)
    shapes = [((ROWS, 8192), BF16), ((1, ROWS, 8192), BF16), ((RANK, BLK), F32)] * 2
    operands = (grad_key, error_key, prev_key.T, grad_val, error_val, prev_val.T)
    held = pl.pallas_call(
        step_kernel,
        name="exchange",
        out_shape=tuple(pltpu.VMEM(*one) for one in shapes),
        in_specs=[hbm] * 6,
        out_specs=(out,) * 6,
        scratch_shapes=scratch,
        compiler_params=pltpu.CompilerParams(
            collective_id=0, has_side_effects=True, vmem_limit_bytes=32 * 2**20
        ),
    )(*(pltpu.with_memory_space_constraint(one, pltpu.HBM) for one in operands))
    uk, nk, fk, uv, nv, fv = pl.pallas_call(
        flush_kernel,
        name="flush",
        out_shape=tuple(jax.ShapeDtypeStruct(*one) for one in shapes),
        in_specs=[pl.BlockSpec(memory_space=pltpu.VMEM)] * 6,
        out_specs=(hbm,) * 6,
        scratch_shapes=[dma((20,))],
        compiler_params=pltpu.CompilerParams(vmem_limit_bytes=2**21),
    )(*(pltpu.with_memory_space_constraint(one, pltpu.VMEM) for one in held))
    return uk, nk, fk.T, uv, nv, fv.T


def solution(mesh):
    wide = P("replica", "shard", None)
    flat = P("shard", None)
    return jax.shard_map(
        per_device,
        mesh=mesh,
        in_specs=(wide, wide, flat, wide, wide, flat),
        out_specs=(flat, wide, flat, flat, wide, flat),
        check_vma=False,
    )
```

```python
import functools

import jax
import jax.numpy as jnp
from jax import lax
from jax.experimental import pallas as pl
from jax.experimental.pallas import tpu as pltpu
from jax.sharding import PartitionSpec as P

MESH = pl.DeviceIdType.MESH
F32, BF16 = jnp.float32, jnp.bfloat16
NX, NY, NZ, NC = 4, 4, 8, 2
REPLICAS = 16
RANK = 64
ROWS = 64
BLK = 512
BLKS = 16
COL = 256
COLS = 32
RIDGE = 1e-6
LAG = 4
NT = (((1,), (1,)), ((), ()))
NN = (((1,), (0,)), ((), ()))


def device(x, y, z, c):
    return (lax.rem(y, 2) * NZ + z, (lax.div(y, 2) * NX + x) * NC + c)


def send(src, dst, ssem, rsem, dev):
    copy = pltpu.make_async_remote_copy(
        src_ref=src, dst_ref=dst, send_sem=ssem, recv_sem=rsem, device_id=dev, device_id_type=MESH
    )
    copy.start()
    return copy


def arrival(dst, ssem, rsem, dev):
    pltpu.make_async_remote_copy(
        src_ref=dst, dst_ref=dst, send_sem=ssem, recv_sem=rsem, device_id=dev, device_id_type=MESH
    ).wait_recv()


def solve_rows(gram, left):
    row = lax.broadcasted_iota(jnp.int32, (RANK, RANK), 0)
    lane = lax.broadcasted_iota(jnp.int32, (RANK, RANK), 1)
    diag = lane == row
    trace = jnp.sum(jnp.where(diag, gram, 0.0))
    rest = (gram + jnp.where(diag, RIDGE * (trace / RANK), 0.0), left)
    sub = lax.broadcasted_iota(jnp.int32, (8, 128), 0)
    done = ([], [])
    for t in range(8):
        count = RANK - 8 * t
        head = [one[:8] for one in rest]
        tail = [one[8:] if t < 7 else None for one in rest]
        cols = [jnp.broadcast_to(rest[0][:, 8 * t + k : 8 * t + k + 1], (count, 128)) for k in range(8)]
        hcol = [col[:8] for col in cols]
        tcol = [col[8:] if t < 7 else None for col in cols]
        for k in range(8):
            inv = pl.reciprocal(hcol[k][k : k + 1, :])
            across = [hcol[j][k : k + 1, :] for j in range(8)]
            pivot = [one[k : k + 1, :] for one in head]
            if k < 7:
                m = jnp.where(sub > k, hcol[k] * inv, 0.0)
                for j in range(k + 1, 8):
                    hcol[j] = hcol[j] - m * across[j]
                head = [head[0] - m[:, :RANK] * pivot[0], head[1] - m * pivot[1]]
            if t < 7:
                m = tcol[k] * inv
                for j in range(k + 1, 8):
                    tcol[j] = tcol[j] - m * across[j]
                tail = [tail[0] - m[:, :RANK] * pivot[0], tail[1] - m * pivot[1]]
        for i in range(2):
            done[i].append(head[i])
        rest = tail
    pivots = jnp.sum(jnp.where(diag, jnp.concatenate(done[0], axis=0), 0.0), axis=1, keepdims=True)
    return jnp.concatenate(done[1], axis=0) * lax.rsqrt(pivots)


def step_kernel(
    gk, ek, pk, gv, ev, pv,
    uk, nk, fk, uv, nv, fv,
    grads, errors, mbuf, mchip, pstage, pbuf, acc, lbuf, r1, lt2, c1, obuf,
    wbuf, s1, r2, s2, r3, s3, r4, fbuf,
    load_sem, token, p_ss, p_rs, m_ss, m_rs, o_ss, o_rs,
    a_ss, a_rs, q_ss, q_rs, b_ss, b_rs, b2_ss, b2_rs, c1_ss, c1_rs,
    e1_ss, e1_rs, e2_ss, e2_rs, e3_ss, e3_rs,
    g3_ss, g3_rs, g2_ss, g2_rs, g1_ss, g1_rs, g0_ss, g0_rs,
):
    r = lax.axis_index("replica")
    s = lax.axis_index("shard")
    y_lo, z = lax.div(r, NZ), lax.rem(r, NZ)
    y_hi, x, c = lax.div(s, NX * NC), lax.rem(lax.div(s, NC), NX), lax.rem(s, NC)
    y = 2 * y_hi + y_lo
    oc = 1 - c
    cross = lax.rem(y + 3 + 2 * y_lo, NY)
    flip = 2 * y_hi + 1 - y_lo
    mate = device(x, y, z, oc)

    def at_x(d):
        return lax.rem(x + d, NX)

    def at_y(d):
        return lax.rem(y + d, NY)

    def at_z(d):
        return lax.rem(z + d, NZ)

    chip = y_hi * NX + x
    own_prev = [
        pltpu.make_async_copy(src.at[pl.ds(32 * h, 32)], pstage.at[m, h], load_sem.at[4 + 2 * m + h])
        for m, src in enumerate((pk, pv))
        for h in range(2)
    ]
    loads = [
        pltpu.make_async_copy(gk.at[0], grads.at[0], load_sem.at[0]),
        pltpu.make_async_copy(ek.at[0], errors.at[0], load_sem.at[1]),
        pltpu.make_async_copy(gv.at[0], grads.at[1], load_sem.at[2]),
        pltpu.make_async_copy(ev.at[0], errors.at[1], load_sem.at[3]),
    ]
    close = (1, 7, 2, 6)
    partners = [device(x, y, at_z(d), c) for d in (2, 6, 1, 7)]
    partners += [device(at_x(d), cross, z, c) for d in (2, 1, 3)]
    partners += [device(at_x(d), y, z, c) for d in (2, 1, 3)]
    partners += [device(x, at_y(d), z, c) for d in (2, 1, 3)]
    partners += [device(at_x(d), cross, z, oc) for d in (2, 1, 3, 0)]
    partners += [device(at_x(d), y, z, oc) for d in (2, 1, 3)]
    partners += [mate]
    barrier = pltpu.get_barrier_semaphore()
    for dev in partners:
        pl.semaphore_signal(barrier, inc=1, device_id=dev, device_id_type=MESH)
    for copy in own_prev + loads:
        copy.start()
    for copy in own_prev:
        copy.wait()
    pl.semaphore_wait(barrier, len(partners))

    sent = []

    def greet(turn):
        for i, d in enumerate(close):
            pl.semaphore_signal(
                token.at[turn, i], inc=1, device_id=device(x, y, at_z(d), c), device_id_type=MESH
            )

    def greeted(turn):
        for i in range(4):
            pl.semaphore_wait(token.at[turn, i], 1)

    def take():
        old = sent[:]
        sent.clear()
        return old

    def settle(copies):
        for copy in copies:
            copy.wait_send()

    far = [(2, 1), (1, 1), (3, 1), (2, 0), (1, 0), (3, 0), (0, 1)]

    def quarter(one, q):
        return pbuf.at[one, lax.rem(q, 4)]

    color = z + 2 * y_lo
    along = c == lax.rem(lax.div(color, 2), 2)
    half = lax.rem(color, 2)
    row = jnp.where(along, y, cross)
    there = quarter(chip, color + jnp.where(along, 0, 2))
    place = jnp.where(along, 3, 0)
    for i in range(3):
        for m in range(2):
            dev = device(at_x(far[i][0]), row, z, m)
            sent.append(send(pstage.at[m, half], there, a_ss.at[m, i], a_rs.at[place + i], dev))

    @pl.when(jnp.logical_not(along))
    def _():
        for m in range(2):
            send(pstage.at[m, half], there, a_ss.at[m, 3], a_rs.at[6], device(x, cross, z, m))

    copy = send(pstage.at[oc], pbuf.at[chip, pl.ds(2 * c, 2)], p_ss, p_rs, mate)
    sent.append(copy)
    pbuf[chip, pl.ds(2 * c, 2)] = pstage[c]
    near = (device(x, flip, z, c), device(x, y, at_z(1), c), device(x, y, at_z(7), c))

    greet(0)
    for copy in loads:
        copy.wait()

    def merge(b, carry):
        cols = pl.ds(pl.multiple_of(b * COL, COL), COL)
        for m in range(2):
            total = grads[m, :, cols].astype(F32) + errors[m, :, cols].astype(F32)
            mbuf[m, b] = total.astype(BF16)
        mchip[c, b] = mbuf[c, b]
        return carry

    lax.fori_loop(0, COLS, merge, 0)
    for t in range(4):
        part = pl.ds(8 * t, 8)
        sent.append(send(mbuf.at[oc, part], mchip.at[c, part], m_ss.at[t], m_rs.at[t], mate))

    greeted(0)
    greet(1)

    def block_of(b):
        return jnp.concatenate([mchip[0, b], mchip[1, b]], axis=0)

    def left_term(one):
        total = None
        for bit in range(2):
            for h in range(2):
                cols = slice(h * COL, h * COL + COL)
                prev = jnp.concatenate([pbuf[one, 2 * bit, :, cols], pbuf[one, 2 * bit + 1, :, cols]], axis=0)
                term = lax.dot_general(prev, block_of(4 * one + 2 * bit + h), NT, preferred_element_type=F32)
                total = term if total is None else total + term
        return total

    order = (4, 5, 6, 1, 2, 3, 0)
    chips = []
    for i, (dx, over) in enumerate(far):
        yy = (1 - y_hi) if over else y_hi
        chips.append(yy * NX + lax.rem(x + NX - dx, NX))
    for i in order:
        piece = quarter(chips[i], color)
        arrival(piece, a_ss.at[i], a_rs.at[i], mate)
        for n in range(3):
            sent.append(send(piece, piece, q_ss.at[i, n], q_rs.at[i, n], near[n]))
    for t in range(4):
        arrival(mchip.at[oc, pl.ds(8 * t, 8)], m_ss.at[t], m_rs.at[t], mate)
    arrival(pbuf.at[chip, pl.ds(2 * oc, 2)], p_ss, p_rs, mate)
    acc[...] = left_term(chip)
    for i in order:
        for n in range(3):
            arrival(quarter(chips[i], color + (2, 3, 1)[n]), q_ss.at[i, n], q_rs.at[i, n], mate)
        acc[...] += left_term(chips[i])

    @pl.when(jnp.logical_not(along))
    def _():
        for m in range(2):
            pltpu.make_async_remote_copy(
                src_ref=pstage.at[m, half], dst_ref=there, send_sem=a_ss.at[m, 3], recv_sem=a_rs.at[6],
                device_id=mate, device_id_type=MESH,
            ).wait_send()

    for t in range(NZ):
        lbuf[t] = acc[8 * t : 8 * t + 8, :]
    r1[r] = lbuf[z]
    greeted(1)
    old = take()
    peers = [(1, d) for d in (4, 3, 5, 2, 6, 1, 7, 0)] + [(0, d) for d in (4, 3, 5, 2, 6, 1, 7)]
    for i, (over, dz) in enumerate(peers):
        dev = device(x, flip if over else y, at_z(dz), c)
        sent.append(send(lbuf.at[at_z(dz)], r1.at[r], b_ss.at[i], b_rs.at[i], dev))
    settle(old)
    for i, (over, dz) in enumerate(peers):
        slot = ((1 - y_lo) if over else y_lo) * NZ + lax.rem(z + NZ - dz, NZ)
        arrival(r1.at[slot], b_ss.at[i], b_rs.at[i], mate)
    total = r1[0]
    for t in range(1, REPLICAS):
        total = total + r1[t]
    lt2[z] = total / REPLICAS
    zs = (4, 3, 5, 2, 6, 1, 7)
    old = take()
    for i, dz in enumerate(zs):
        sent.append(send(lt2.at[z], lt2.at[z], b2_ss.at[i], b2_rs.at[i], device(x, y, at_z(dz), c)))
    settle(old)
    for i, dz in enumerate(zs):
        arrival(lt2.at[lax.rem(z + NZ - dz, NZ)], b2_ss.at[i], b2_rs.at[i], mate)

    left = jnp.concatenate([lt2[t] for t in range(NZ)], axis=0)
    gram = lax.dot_general(left, left, NT, precision=lax.Precision.HIGHEST, preferred_element_type=F32)
    c1[chip] = jnp.concatenate([gram[0:32], gram[32:64]], axis=1)
    old = take()
    for i, (dx, over) in enumerate(far):
        dev = device(at_x(dx), cross if over else y, z, c)
        sent.append(send(c1.at[chip], c1.at[chip], c1_ss.at[i], c1_rs.at[i], dev))
    settle(old)
    for i in range(7):
        arrival(c1.at[chips[i]], c1_ss.at[i], c1_rs.at[i], mate)
    total = c1[0]
    for t in range(1, 8):
        total = total + c1[t]
    gram = jnp.concatenate([total[:, :RANK], total[:, RANK:]], axis=0)

    ortho = solve_rows(gram, left).astype(BF16)
    obuf[c] = ortho
    old = take()
    copy = send(obuf.at[c], obuf.at[c], o_ss, o_rs, mate)
    sent.append(copy)

    firsts = (x, y)
    seconds = (y, x)
    ds = (2, 1, 3, 0)

    def first(pq, d):
        return lax.rem(firsts[pq] + d, 4)

    def second(pq, d):
        return lax.rem(seconds[pq] + d, 4)

    def dev1(pq, d):
        return device(at_x(d), y, z, c) if pq == 0 else device(x, at_y(d), z, c)

    def dev2(pq, d):
        return device(x, at_y(d), z, c) if pq == 0 else device(at_x(d), y, z, c)

    for j, dj in enumerate(ds):
        for pq in range(2):
            i2 = second(pq, dj)
            for k, dk in enumerate(ds):
                block = block_of(pq * 16 + first(pq, dk) * 4 + i2)
                term = lax.dot_general(ortho, block, NN, preferred_element_type=F32)
                for a in range(4):
                    for b in range(2):
                        tile = term[16 * a : 16 * a + 16, b * 128 : b * 128 + 128]
                        if dk == 0:
                            wbuf[pq, j, 2 * a + b] = tile
                        else:
                            s1[pq, j, k, 2 * a + b] = tile.astype(BF16)
                if dk != 0:
                    sent.append(
                        send(s1.at[pq, j, k], r2.at[pq, j, k], e1_ss.at[pq, j, k], e1_rs.at[pq, j, k], dev1(pq, dk))
                    )
    settle(old)
    for j, dj in enumerate(ds):
        for pq in range(2):
            total = wbuf[pq, j]
            for k in range(3):
                arrival(r2.at[pq, j, k], e1_ss.at[pq, j, k], e1_rs.at[pq, j, k], mate)
                total = total + r2[pq, j, k].astype(F32)
            if dj == 0:
                wbuf[pq, j] = total
            else:
                s2[pq, j] = total.astype(BF16)
                sent.append(
                    send(s2.at[pq, j], r3.at[pq, j], e2_ss.at[pq, j], e2_rs.at[pq, j], dev2(pq, dj))
                )
    settle(take())
    for pq in range(2):
        total = wbuf[pq, 3]
        for j in range(3):
            arrival(r3.at[pq, j], e2_ss.at[pq, j], e2_rs.at[pq, j], mate)
            total = total + r3[pq, j].astype(F32)
        wbuf[pq, 3] = total
        s3[:, pq] = total.astype(BF16)
    old = take()
    for i, dz in enumerate(zs):
        there = at_z(dz)
        sent.append(send(s3.at[there], r4.at[i], e3_ss.at[i], e3_rs.at[i], device(x, y, there, c)))
    settle(old)
    last = take()
    for i in range(7):
        arrival(r4.at[i], e3_ss.at[i], e3_rs.at[i], mate)
    for pq in range(2):
        i1, i2 = first(pq, 0), second(pq, 0)
        total = wbuf[pq, 3, z]
        for i in range(7):
            total = total + r4[i, pq].astype(F32)
        fbuf[c, pq, i1, i2, z] = (total / REPLICAS).astype(BF16)

    for pq in range(2):
        piece = fbuf.at[c, pq, first(pq, 0), second(pq, 0), z]
        for i, dz in enumerate(zs):
            sent.append(send(piece, piece, g3_ss.at[pq, i], g3_rs.at[pq, i], device(x, y, at_z(dz), c)))
    settle(last)
    last = take()
    arrival(obuf.at[oc], o_ss, o_rs, mate)
    wide = []
    for m in range(2):
        turned = obuf[m].astype(F32).T
        turned = jnp.where(c == 0, turned[:ROWS], turned[ROWS:])
        none = jnp.zeros((ROWS, RANK), F32)
        wide.append(jnp.concatenate([turned, none] if m == 0 else [none, turned], axis=1))
    wide = jnp.concatenate(wide, axis=0).astype(BF16)

    def sub_piece(pq, k, j):
        return fbuf.at[c, pq, first(pq, 4 - ds[k]), second(pq, 4 - ds[j])]

    def pass_on(pq, k, j):
        piece = sub_piece(pq, k, j)
        sent.append(send(piece, piece, g0_ss.at[pq, k, j], g0_rs.at[pq, k, j], mate))
        chunks.append((pq, k, j))

    def spread(pq, j):
        piece = sub_piece(pq, 3, j)
        for k in range(3):
            sent.append(send(piece, piece, g1_ss.at[pq, j, k], g1_rs.at[pq, j, k], dev1(pq, ds[k])))
        pass_on(pq, 3, j)

    def finish(pq, k, j):
        i1, i2 = first(pq, 4 - ds[k]), second(pq, 4 - ds[j])
        arrival(fbuf.at[oc, pq, i1, i2], g0_ss.at[pq, k, j], g0_rs.at[pq, k, j], mate)
        sides = []
        for m in range(2):
            tiles = fbuf[m, pq, i1, i2]
            rows = [jnp.concatenate([tiles[2 * a], tiles[2 * a + 1]], axis=1) for a in range(4)]
            sides.append(jnp.concatenate(rows, axis=0))
        factor = jnp.concatenate(sides, axis=0)
        approx = lax.dot_general(wide, factor, NN, preferred_element_type=F32)
        block = pq * 16 + i1 * 4 + i2
        merged = jnp.concatenate([mbuf[0, block], mbuf[1, block]], axis=0)
        rest = (merged.astype(F32) - approx).astype(BF16)
        approx = approx.astype(BF16)
        cols = pl.ds(pl.multiple_of(block * COL, COL), COL)
        for m, (u, e) in enumerate(((uk, nk), (uv, nv))):
            u[:, cols] = approx[m * ROWS : m * ROWS + ROWS]
            e[0, :, cols] = rest[m * ROWS : m * ROWS + ROWS]

    def settle_some():
        for _ in range(min(3, len(sent) - 6)):
            sent.pop(0).wait_send()

    chunks = []
    for pq in range(2):
        piece = sub_piece(pq, 3, 3)
        for i, dz in enumerate(zs):
            arrival(
                fbuf.at[c, pq, first(pq, 0), second(pq, 0), lax.rem(z + NZ - dz, NZ)],
                g3_ss.at[pq, i], g3_rs.at[pq, i], mate,
            )
        for k in range(3):
            sent.append(send(piece, piece, g2_ss.at[pq, k], g2_rs.at[pq, k], dev2(pq, ds[k])))
        spread(pq, 3)
    settle(last)
    for j in (1, 2, 0):
        for pq in range(2):
            arrival(sub_piece(pq, 3, j), g2_ss.at[pq, j], g2_rs.at[pq, j], mate)
            spread(pq, j)
    for j in (3, 1, 2, 0):
        for pq in range(2):
            for k in (1, 2, 0):
                arrival(sub_piece(pq, k, j), g1_ss.at[pq, j, k], g1_rs.at[pq, j, k], mate)
                pass_on(pq, k, j)
                settle_some()
                if len(chunks) > LAG:
                    finish(*chunks.pop(0))
    while chunks:
        settle_some()
        finish(*chunks.pop(0))
    for i in range(2):
        for m in range(2):
            rows = [
                jnp.concatenate([fbuf[m, s // 8, s % 8 // 2, s % 2 * 2 + i, 2 * a + b] for b in range(2)], axis=1)
                for a in range(4)
            ]
            (fk, fv)[m][:, i * COL : (i + 1) * COL] = jnp.concatenate(rows, axis=0).astype(F32)
    for copy in sent:
        copy.wait_send()


def flush_kernel(uk, nk, fk, uv, nv, fv, uk_out, nk_out, fk_out, uv_out, nv_out, fv_out, sems):
    pairs = [(fk, fk_out), (fv, fv_out)]
    for q in range(4):
        rows = pl.ds(16 * q, 16)
        pairs += [(uk.at[rows], uk_out.at[rows]), (uv.at[rows], uv_out.at[rows])]
        pairs += [(nk.at[0, rows], nk_out.at[0, rows]), (nv.at[0, rows], nv_out.at[0, rows])]
    copies = [pltpu.make_async_copy(src, dst, sems.at[i]) for i, (src, dst) in enumerate(pairs)]
    for copy in copies:
        copy.start()
    for copy in copies:
        copy.wait()


def per_device(grad_key, error_key, prev_key, grad_val, error_val, prev_val):
    vm = pltpu.VMEM
    dma = pltpu.SemaphoreType.DMA
    scratch = [
        vm((2, ROWS, 8192), BF16), vm((2, ROWS, 8192), BF16),
        vm((2, COLS, ROWS, COL), BF16), vm((2, COLS, ROWS, COL), BF16),
        vm((2, 2, 32, BLK), BF16), vm((8, 4, 32, BLK), BF16),
        vm((RANK, 128), F32), vm((8, 8, 128), F32), vm((16, 8, 128), F32), vm((8, 8, 128), F32),
        vm((8, 32, 128), F32), vm((2, RANK, 128), BF16),
        vm((2, 4, 8, 16, 128), F32),
        vm((2, 4, 3, 8, 16, 128), BF16), vm((2, 4, 3, 8, 16, 128), BF16),
        vm((2, 3, 8, 16, 128), BF16), vm((2, 3, 8, 16, 128), BF16),
        vm((8, 2, 16, 128), BF16), vm((7, 2, 16, 128), BF16),
        vm((2, 2, 4, 4, 8, 16, 128), BF16),
        dma((8,)), pltpu.SemaphoreType.REGULAR((2, 4)),
    ]
    for n in (
        None, None, (4,), (4,), None, None, (2, 4), (7,), (7, 3), (7, 3), (15,), (15,), (7,), (7,), (7,), (7,),
        (2, 4, 3), (2, 4, 3), (2, 3), (2, 3), (7,), (7,),
        (2, 7), (2, 7), (2, 3), (2, 3), (2, 4, 3), (2, 4, 3), (2, 4, 4), (2, 4, 4),
    ):
        scratch.append(dma if n is None else dma(n))
    hbm = pl.BlockSpec(memory_space=pl.ANY)
    out = pl.BlockSpec(memory_space=pltpu.VMEM)
    shapes = [((ROWS, 8192), BF16), ((1, ROWS, 8192), BF16), ((RANK, BLK), F32)] * 2
    operands = (grad_key, error_key, prev_key.T, grad_val, error_val, prev_val.T)
    held = pl.pallas_call(
        step_kernel,
        name="exchange",
        out_shape=tuple(pltpu.VMEM(*one) for one in shapes),
        in_specs=[hbm] * 6,
        out_specs=(out,) * 6,
        scratch_shapes=scratch,
        compiler_params=pltpu.CompilerParams(
            collective_id=0, has_side_effects=True, vmem_limit_bytes=32 * 2**20
        ),
    )(*(pltpu.with_memory_space_constraint(one, pltpu.HBM) for one in operands))
    uk, nk, fk, uv, nv, fv = pl.pallas_call(
        flush_kernel,
        name="flush",
        out_shape=tuple(jax.ShapeDtypeStruct(*one) for one in shapes),
        in_specs=[pl.BlockSpec(memory_space=pltpu.VMEM)] * 6,
        out_specs=(hbm,) * 6,
        scratch_shapes=[dma((20,))],
        compiler_params=pltpu.CompilerParams(vmem_limit_bytes=2**21),
    )(*(pltpu.with_memory_space_constraint(one, pltpu.VMEM) for one in held))
    return uk, nk, fk.T, uv, nv, fv.T


def solution(mesh):
    wide = P("replica", "shard", None)
    flat = P("shard", None)
    return jax.shard_map(
        per_device,
        mesh=mesh,
        in_specs=(wide, wide, flat, wide, wide, flat),
        out_specs=(flat, wide, flat, flat, wide, flat),
        check_vma=False,
    )
```
